32 devices in a mesh: comp: 2 (over x), dom: 16 (over z, y, core).
Axes of the slice: x: 2, y: 2, z: 4, core: 2. Of those that a mesh axis runs over, the one named last changes fastest.
Arguments:
- state: float32 [2, 16, 262144], P('comp', None, 'dom'), may hold values from -6 to 6
- export_fields: float32 [2, 8, 262144], P('comp', None, 'dom'), may hold values from -6 to 6
- remap_weights: float32 [2, 2048, 128, 128], P('comp', 'dom'), may hold values from -0.5 to 0.5
- routes: int32 [2, 2048, 1], P('comp', 'dom'), may hold values from 0 to 15; in each aligned block of 128 rows (0 to 127, 128 to 255, ..., all dimensions but the last counted through in order) at most 16 rows name the same one
- target_block: int32 [2, 2048], P('comp', 'dom'), may hold values from 0 to 127
- source_block: int32 [2, 2048], P('comp', 'dom'), may hold values from 0 to 127
- wet_mask: int32 [2, 262144], P('comp', 'dom'), may hold values 0 or 1
- edge_coeff: float32 [2, 6, 262144], P('comp', None, 'dom'), may hold values from 0.02 to 0.15
- edge_offset: int32 [2, 6, 262144], P('comp', None, 'dom'), may hold values from -256 to 256
- vert_coeff: float32 [2, 15, 262144], P('comp', None, 'dom'), may hold values from 0.1 to 10
Outputs:
- new_state: float32 [2, 16, 262144], P('comp', None, 'dom')
- imported: float32 [2, 8, 262144], P('comp', None, 'dom')
The draws below stay inside these ranges and needn't reach their ends.
Inputs may be any that keep to these rules, and one draw needn't show every extreme that they name: `routes`: in each device's 128 remap blocks no owner is named by more than 16 blocks, a bound that some block reaches.
All inputs are finite; a program needn't handle non-finite values. No bound on the sum of `wet_mask` on one device may be relied on, other than what follows from the above.
Results may differ from the reference program's by a relative error of at most 0.0001.
Values sent between devices are 32-bit elements; how exact they have to be, the bound alone decides.
No kernel may reach another device: no remote copies, remote signals or barrier semaphores. Data moves between devices by JAX's collectives and lax.ppermute only.
A program may use at most 192 MiB of HBM per device.

```python
import math
import jax
import jax.numpy as jnp
import numpy as np
from jax import lax

LEV = 16
NF = 8
NB = 6
TB = 128
RIM = 256
STEPS = 4
NBLK = 128
CAP = 16
NC = 262144
N_DOM = 16


def plant(drawn, key, least, largest):
    extent = drawn.shape
    place = [jax.random.randint(jax.random.fold_in(key, axis), (), 0, extent[axis]) for axis in range(len(extent))]
    drawn = drawn.at[tuple(place)].set(least)
    longest = extent.index(max(extent))
    place[longest] = (place[longest] + 1) % extent[longest]
    return drawn.at[tuple(place)].set(largest)


def level_of(rng, dims, shards, least, high):
    gain, own = 1.0, jax.random.fold_in(rng, 6)
    for position, blocks in shards:
        draws = jnp.exp(jax.random.uniform(jax.random.fold_in(own, position), (blocks,), jnp.float32, least / len(shards), high / len(shards)))
        gain = gain * jnp.repeat(draws, dims[position] // blocks).reshape([-1 if axis == position else 1 for axis in range(len(dims))])
    return gain


def deal_out(own_key, own, number, rows, number_of, top, limit, lean):
    ranking = jax.random.permutation(own_key, number_of)
    heavy_load, common = portions_of(number_of, rows * top, limit, lean, True), portions_of(number_of, rows * top, limit, lean, False)
    places = jnp.arange(number_of)

    def named(sizes, turn):
        used = int((sizes > 0).sum())
        fixed = max(1, used // 4)
        passed = fixed + (places - fixed + turn * (used - fixed)) % max(1, number_of - fixed)
        return jnp.zeros((number_of,), jnp.int32).at[ranking[jnp.where(places < fixed, places, passed)]].set(jnp.asarray(sizes, jnp.int32))

    sizes = jnp.where(number % 4 == 0, named(heavy_load, number // 4), named(common, number - number // 4 - 1))
    mixed = jax.random.permutation(jax.random.fold_in(own, 3), number_of)
    source_of, taker = mixed[0:number_of // 2 * 2:2], mixed[1:number_of // 2 * 2:2]
    room = jnp.minimum(sizes[source_of] - 1, limit - sizes[taker]) // 2
    room = jnp.where((source_of == ranking[0]) | (taker == ranking[0]) | (sizes[taker] == 0), 0, jnp.maximum(room, 0))
    passed = jax.random.randint(jax.random.fold_in(own, 4), (number_of // 2,), 0, 1 << 20) % (room + 1)
    sizes = sizes.at[source_of].add(-passed).at[taker].add(passed)
    members = jnp.searchsorted(jnp.cumsum(sizes), jnp.arange(rows * top), side="right").astype(jnp.int32)
    listing = members.reshape(top, rows).T
    listing = listing[jax.random.permutation(jax.random.fold_in(own, 1), rows)]
    turn = jax.random.randint(jax.random.fold_in(own, 2), (rows, 1), 0, top)
    return jnp.take_along_axis(listing, (jnp.arange(top)[None, :] + turn) % top, axis=1)


def portions_of(amount, total, bound, slope, full):
    portions = [(1 << 20) // math.isqrt(standing ** slope) + 1 for standing in range(1, amount + 1)]
    largest = bound if full else min(bound, max(-(-total // amount), total * portions[0] // sum(portions)))
    least = 1 if total - largest >= amount - 1 else 0
    counts, surplus = [largest] + [least] * (amount - 1), total - largest - least * (amount - 1)
    while surplus > 0:
        movable = [i for i in range(1, amount) if counts[i] < largest] or [i for i in range(1, amount) if counts[i] < bound]
        whole, budget = sum([portions[i] for i in movable]), surplus
        for i in movable:
            more = min(bound - counts[i], max(1, budget * portions[i] // whole), surplus)
            counts[i] = counts[i] + more
            surplus = surplus - more
    return np.array(counts)


def normal_values(key, extent, scale, bound, pieces=(), kind=jnp.bfloat16):
    level = level_of(key, extent, pieces, -0.22, 0.18) if pieces else 1.0
    values = jax.random.normal(key, extent, jnp.float32) * scale * level
    return jnp.minimum(jnp.maximum(values, -bound), bound).astype(kind)


def setup_inputs(seed: int = 0) -> dict:
    streams_of = jax.random.split(jax.random.key(seed), 11)
    state = normal_values(streams_of[0], (2, LEV, NC), 1.0, 6.0, ((0, 2), (2, 16)), jnp.float32)
    export_fields = normal_values(streams_of[1], (2, NF, NC), 1.0, 6.0, ((0, 2), (2, 16)), jnp.float32)
    remap_weights = normal_values(streams_of[2], (2, NC // TB, TB, TB), TB ** -0.5, 0.5, ((0, 2), (1, 16)), jnp.float32)
    routes_keys = jax.random.split(jax.random.fold_in(streams_of[3], 1), 2 * (NC // TB) // NBLK)
    routes_turns = jax.random.permutation(jax.random.fold_in(streams_of[3], 3), 2 * (NC // TB) // NBLK)
    routes = jax.vmap(lambda own, number: deal_out(jax.random.fold_in(streams_of[3], 2), own, number, NBLK, N_DOM, 1, CAP, 2))(routes_keys, routes_turns).reshape((2, NC // TB, 1))
    target_block = plant(jax.random.randint(streams_of[4], (2, NC // TB), 0, NBLK), jax.random.fold_in(streams_of[4], 1), 0, NBLK - 1).astype(jnp.int32)
    source_block = plant(jax.random.randint(streams_of[5], (2, NC // TB), 0, NBLK), jax.random.fold_in(streams_of[5], 1), 0, NBLK - 1).astype(jnp.int32)
    wet_mask = plant((jax.random.randint(streams_of[6], (2, NC), 0, 4) < 3).astype(jnp.int32), jax.random.fold_in(streams_of[6], 1), 0, 1)
    edge_coeff = jnp.clip(0.02 + 0.13000001 * jax.random.uniform(streams_of[7], (2, NB, NC), jnp.float32) ** level_of(streams_of[7], (2, NB, NC), ((0, 2), (2, 16)), -0.2, 0.2), 0.02, 0.15)
    edge_offset = plant(jax.random.randint(streams_of[8], (2, NB, NC), 0 - RIM, RIM + 1), jax.random.fold_in(streams_of[8], 1), 0 - RIM, RIM).astype(jnp.int32)
    vert_coeff = jnp.clip(jnp.exp(math.log(10.0) - 4.6051702 * jax.random.uniform(streams_of[9], (2, LEV - 1, NC), jnp.float32) ** level_of(streams_of[9], (2, LEV - 1, NC), ((0, 2), (2, 16)), -0.2, 0.2)), 0.1, 10.0)
    return dict(state=state, export_fields=export_fields, remap_weights=remap_weights, routes=routes, target_block=target_block, source_block=source_block, wet_mask=wet_mask, edge_coeff=edge_coeff, edge_offset=edge_offset, vert_coeff=vert_coeff)


force_scale = 0.5


def factor_column(vert):
    upper_coef = jnp.concatenate([jnp.zeros_like(vert[:1]), vert], axis=0)
    lower_coef = jnp.concatenate([vert, jnp.zeros_like(vert[:1])], axis=0)
    diagonal = 1.0 + upper_coef + lower_coef

    def advance(previous, levels):
        diag_row, upper_row, lower_row = levels
        pivots = diag_row + upper_row * previous
        ratio = -lower_row / pivots
        return ratio, (ratio, pivots)

    unused_last, (ratios, pivots) = lax.scan(advance, jnp.zeros_like(vert[0]), (diagonal, upper_coef, lower_coef))
    return upper_coef, ratios, pivots


def solve_column(right_hand, factors):
    upper_coef, ratios, pivots = factors

    def forward(previous, levels):
        rhs_row, upper_row, pivot_row = levels
        value = (rhs_row + upper_row * previous) / pivot_row
        return value, value

    def backward(following, levels):
        partial_row, ratio_row = levels
        value = partial_row - ratio_row * following
        return value, value

    unused_one, partial_value = lax.scan(forward, jnp.zeros_like(right_hand[0]), (right_hand, upper_coef, pivots))
    unused_two, solved = lax.scan(backward, jnp.zeros_like(right_hand[0]), (partial_value, ratios), reverse=True)
    return solved


def remap_from(sender_export, sender_weights, sender_routes, sender_target, sender_source):
    width, total = sender_export.shape
    blocks = sender_export.reshape(width, total // TB, TB)
    rows = jnp.arange(sender_source.shape[0], dtype=jnp.int32)
    global_source = (rows // NBLK) * NBLK + sender_source
    picked = jnp.transpose(blocks[:, global_source, :], (1, 0, 2))
    mapped = jnp.einsum("bft,bts->bfs", picked, sender_weights, precision=lax.Precision.HIGHEST)
    global_target = sender_routes[:, 0] * NBLK + sender_target
    summed = jax.ops.segment_sum(mapped, global_target, num_segments=total // TB)
    return jnp.transpose(summed, (1, 0, 2)).reshape(width, total)


def advance_component(column_state, incoming, wet_row, edge_row, offset_row, vert_row):
    total = column_state.shape[1]
    neighbours = (jnp.arange(total, dtype=jnp.int32)[None, :] + offset_row) % total
    forcing = incoming * wet_row[None, :].astype(jnp.float32) * force_scale
    factors = factor_column(vert_row)
    for substep in range(STEPS):
        spread = jnp.zeros_like(column_state)
        for which in range(NB):
            spread = spread + edge_row[which][None, :] * (column_state[:, neighbours[which]] - column_state)
        right_hand = column_state + spread
        right_hand = right_hand.at[:NF].add(forcing)
        column_state = solve_column(right_hand, factors)
    return column_state


def reference(state, export_fields, remap_weights, routes, target_block, source_block, wet_mask, edge_coeff, edge_offset, vert_coeff):
    results = []
    imports = []
    for comp_id in range(2):
        sender = 1 - comp_id
        incoming = remap_from(export_fields[sender], remap_weights[sender], routes[sender], target_block[sender], source_block[sender])
        imports.append(incoming)
        results.append(advance_component(state[comp_id], incoming, wet_mask[comp_id], edge_coeff[comp_id], edge_offset[comp_id], vert_coeff[comp_id]))
    return jnp.stack(results), jnp.stack(imports)
```

```python
import functools

import jax
import jax.numpy as jnp
from jax import lax
from jax.experimental import pallas as pl
from jax.experimental.pallas import tpu as pltpu
from jax.sharding import PartitionSpec as P

NB = 6
RIM = 256
STEPS = 4
LANES = 128
REACH = RIM // LANES
HALO = STEPS * REACH
PAD = 8
MIB = 2**20
CHUNK = 3 * 8

force_scale = 0.5

F32 = jnp.float32
BF16 = jnp.bfloat16


def split(value):
    high = value.astype(BF16)
    return high, (value - high.astype(F32)).astype(BF16)


def remap_kernel(
    owners, capacity, routes, target, source, me, fields, weights, *refs
):
    edges, (out, low, high, counts) = refs[:10], refs[10:]
    step = pl.program_id(0)
    per_step = weights.shape[0]
    width = fields.shape[0]
    lane = lax.broadcasted_iota(jnp.int32, (1, LANES), 1)
    label_row = capacity * width

    @pl.when(step == 0)
    def _():
        out[...] = jnp.zeros_like(out)
        for owner in range(owners):
            counts[owner] = 0
        for side, pack in ((0, low), (1, high)):
            state, coef, offset, vert, wet = edges[side::2]
            levels = state.shape[0]
            for row in range(HALO):
                for level in range(0, levels, 8):
                    tile = state[level : level + 8, row * LANES : (row + 1) * LANES]
                    pack[pl.ds(level * HALO + row, 8, stride=HALO), :] = tile
            at = levels * HALO
            for part in (coef, offset, vert):
                for index in range(part.shape[0]):
                    pack[at : at + HALO, :] = part[index].astype(F32)
                    at += HALO
            pack[at : at + HALO, :] = wet[...].astype(F32)

    for local_block in range(per_step):
        block = step * per_step + local_block
        owner = routes[block]
        rank = counts[owner]
        counts[owner] = rank + 1
        start = pl.multiple_of(source[block] * LANES, LANES)
        picked_high, picked_low = split(fields[:, pl.ds(start, LANES)])
        picked = jnp.concatenate([picked_high, picked_low], axis=0)
        high_part, low_part = split(weights[local_block])
        by_high = jnp.dot(picked, high_part, preferred_element_type=F32)
        by_low = jnp.dot(picked, low_part, preferred_element_type=F32)
        value = (by_low[:width] + by_low[width:] + by_high[width:]) + by_high[:width]
        row = pl.multiple_of(rank * width, width)
        out[owner, pl.ds(row, width), :] = value
        slot = lax.rem(me[0] * capacity + rank, LANES)
        old = out[owner, label_row : label_row + 1, :]
        out[owner, label_row : label_row + 1, :] = jnp.where(
            lane == slot, (target[block] + 1).astype(F32), old
        )


def remap(routes, target, source, me, fields, weights, state, parts, owners, capacity):
    block_count = weights.shape[0]
    width, cells = fields.shape
    levels = state.shape[0]
    rows = cells // LANES
    per_step = 16
    edge = HALO * LANES
    ends = (rows // HALO - 1, 0)
    specs = [pl.BlockSpec((levels, edge), lambda i, *_, e=e: (0, e)) for e in ends]
    edges = [state, state]
    pack_rows = levels * HALO
    for part in parts:
        if part.ndim == 3:
            count = part.shape[0]
            specs += [
                pl.BlockSpec((count, HALO, LANES), lambda i, *_, e=e: (0, e, 0)) for e in ends
            ]
        else:
            count = 1
            specs += [pl.BlockSpec((HALO, LANES), lambda i, *_, e=e: (e, 0)) for e in ends]
        pack_rows += count * HALO
        edges += [part, part]
    slots = (owners, capacity * width + 8, LANES)
    return pl.pallas_call(
        functools.partial(remap_kernel, owners, capacity),
        grid_spec=pltpu.PrefetchScalarGridSpec(
            num_scalar_prefetch=4,
            grid=(block_count // per_step,),
            in_specs=[
                pl.BlockSpec((width, cells), lambda i, *_: (0, 0)),
                pl.BlockSpec((per_step, LANES, LANES), lambda i, *_: (i, 0, 0)),
                *specs,
            ],
            out_specs=[
                pl.BlockSpec(slots, lambda i, *_: (0, 0, 0)),
                pl.BlockSpec((pack_rows, LANES), lambda i, *_: (0, 0)),
                pl.BlockSpec((pack_rows, LANES), lambda i, *_: (0, 0)),
            ],
            scratch_shapes=[pltpu.SMEM((owners,), jnp.int32)],
        ),
        out_shape=[
            jax.ShapeDtypeStruct(slots, F32),
            jax.ShapeDtypeStruct((pack_rows, LANES), F32),
            jax.ShapeDtypeStruct((pack_rows, LANES), F32),
        ],
        compiler_params=pltpu.CompilerParams(vmem_limit_bytes=60 * MIB),
        name="remap",
    )(routes, target, source, me, fields, weights, *edges)


def assemble_kernel(owners, capacity, width, slots, out, low, high, hot, values):
    rows = out.shape[1]
    count = owners * capacity
    per_row = LANES // capacity
    size = capacity * width
    pitch = size + 8
    block = lax.broadcasted_iota(jnp.int32, (rows, LANES), 0) + 1
    for sender in range(owners):
        values[sender * size : (sender + 1) * size, :] = slots[
            sender * pitch : sender * pitch + size, :
        ]
    for half in range(count // LANES):
        label = None
        for sender in range(half * per_row, (half + 1) * per_row):
            row = slots[sender * pitch + size : sender * pitch + size + 1, :]
            label = row if label is None else label + row
        label = jnp.broadcast_to(label.astype(jnp.int32), (rows, LANES))
        hot[:, half * LANES : (half + 1) * LANES] = (label == block).astype(F32).astype(BF16)
    picks = hot[...]
    for field in range(width):
        value_high, value_low = split(values[pl.ds(field, count, stride=width), :])
        both = jnp.concatenate([value_high, value_low], axis=1)
        total = jnp.dot(picks, both, preferred_element_type=F32)
        total = total[:, :LANES] + total[:, LANES:]
        out[field] = total
        low[field] = total[:HALO]
        high[field] = total[rows - HALO :]


def assemble(slots, owners, capacity, width, rows):
    return pl.pallas_call(
        functools.partial(assemble_kernel, owners, capacity, width),
        out_shape=[
            jax.ShapeDtypeStruct((width, rows, LANES), F32),
            jax.ShapeDtypeStruct((width, HALO, LANES), F32),
            jax.ShapeDtypeStruct((width, HALO, LANES), F32),
        ],
        scratch_shapes=[
            pltpu.VMEM((rows, owners * capacity), BF16),
            pltpu.VMEM((owners * capacity * width, LANES), F32),
        ],
        compiler_params=pltpu.CompilerParams(vmem_limit_bytes=12 * MIB),
        name="assemble",
    )(slots)


def lane_pick(value, index):
    return jnp.take_along_axis(value, index, axis=1, mode="promise_in_bounds")


def to_lanes(levels, total, column, wide):
    pitch = column.shape[0] // levels

    @pl.loop(0, total, unroll=8)
    def _(row):
        here = pl.ds(pl.multiple_of((row + PAD) * LANES, LANES), LANES)
        tiles = [
            column[pl.ds(level * pitch + PAD + row, 8, stride=pitch), :]
            for level in range(0, levels, 8)
        ]
        high, low = split(jnp.concatenate(tiles, axis=0))
        wide[0:levels, here] = high
        wide[levels : 2 * levels, here] = low


def spread(levels, total, column, wide, matrix, lanes, codes, coefs, mix):
    pitch = column.shape[0] // levels
    span = (2 * REACH + 1) * LANES

    @pl.loop(0, total // CHUNK)
    def _(chunk):
        base = pl.multiple_of(chunk * CHUNK, 8)
        for tile in range(CHUNK - 8):
            row = base + tile
            at = pl.multiple_of((row + PAD - REACH) * LANES, LANES)
            got = jnp.dot(
                wide[:, pl.ds(at, span)],
                matrix[chunk * (CHUNK - 8) + tile],
                preferred_element_type=F32,
            )
            got = got[:, :LANES] + got[:, LANES:]
            got = got[:levels] + got[levels:]
            for level in range(0, levels, 8):
                mix[pl.ds(level * total + row, 8, stride=total), :] = got[level : level + 8]
        row = base + CHUNK - 8
        here = pl.ds(row, 8)
        right = [None] * levels
        for which in range(NB):
            index = lanes[which, here, :]
            code = codes[which, here, :]
            factor = coefs[which, here, :]
            for level in range(levels):
                found = None
                for reach in range(2 * REACH + 1):
                    at = level * pitch + PAD - REACH + reach + row
                    picked = lane_pick(column[pl.ds(at, 8), :], index)
                    found = picked if found is None else jnp.where(code == reach, picked, found)
                found = factor * found
                right[level] = found if which == 0 else right[level] + found
        for level in range(levels):
            mix[pl.ds(level * total + row, 8), :] = right[level]


def prepare_kernel(
    state, coef, offset, vert, wet, low, high,
    column, mix, matrix, inv, from_up, from_down, lanes, codes, coefs, keep, wets,
    wide, places, merged, verts,
):
    levels = state.shape[0]
    rows = state.shape[1] // LANES
    total = rows + 2 * HALO
    pitch = column.shape[0] // levels
    inner = levels - 1

    for pack, first in ((low, 0), (high, total - HALO)):
        for level in range(levels):
            at = level * pitch + PAD + first
            column[at : at + HALO, :] = pack[level * HALO : (level + 1) * HALO, :]
        here = slice(first, first + HALO)
        at = levels * HALO
        for out, count in ((coefs, NB), (places, NB), (verts, inner)):
            for index in range(count):
                out[index, here, :] = pack[at : at + HALO, :].astype(out.dtype)
                at += HALO
        wets[here, :] = pack[at : at + HALO, :] * force_scale
    main = slice(HALO, HALO + rows)
    coefs[:, main, :] = coef[...]
    places[:, main, :] = offset[...]
    verts[:, main, :] = vert[...]
    wets[main, :] = wet[...].astype(F32) * force_scale

    @pl.loop(0, rows, unroll=8)
    def _(row):
        here = pl.ds(pl.multiple_of(row * LANES, LANES), LANES)
        for level in range(0, levels, 8):
            at = level * pitch + PAD + HALO + row
            column[pl.ds(at, 8, stride=pitch), :] = state[level : level + 8, here]

    to_lanes(levels, total, column, wide)
    lane = lax.broadcasted_iota(jnp.int32, (8, LANES), 1)

    @pl.loop(0, total // 8)
    def _(group):
        here = pl.ds(pl.multiple_of(group * 8, 8), 8)
        spots = [places[which, here, :] + lane + RIM for which in range(NB)]
        factors = [coefs[which, here, :] for which in range(NB)]
        left = 1.0
        for which in range(NB):
            places[which, here, :] = spots[which]
            lanes[which, here, :] = jnp.bitwise_and(spots[which], LANES - 1)
            codes[which, here, :] = lax.shift_right_logical(spots[which], 7)
            left = left - factors[which]
            joint = factors[which]
            for other in range(NB):
                if other != which:
                    joint = joint + jnp.where(spots[other] == spots[which], factors[other], 0.0)
            merged[which, here, :] = joint
        keep[here, :] = left
        upper = jnp.zeros((8, LANES), F32)
        carried = jnp.zeros((8, LANES), F32)
        for level in range(levels):
            lower = verts[level, here, :] if level < inner else jnp.zeros((8, LANES), F32)
            pivot = (1.0 + upper + lower) - upper * carried
            inverse = 1.0 / pivot
            carried = lower * inverse
            inv[level, here, :] = inverse
            from_up[level, here, :] = upper * inverse
            from_down[level, here, :] = carried
            upper = lower

    span = (2 * REACH + 1) * LANES
    small = jnp.int16

    @pl.loop(0, total // CHUNK)
    def _(chunk):
        @pl.loop(0, CHUNK - 8)
        def _(tile):
            row = chunk * CHUNK + tile
            at = chunk * (CHUNK - 8) + tile
            spots, highs, lows = [], [], []
            for which in range(NB):
                spot = places[which, pl.ds(row, 1), :]
                spots.append(jnp.broadcast_to(spot, (16, LANES)).astype(small))
                joint_high, joint_low = split(
                    jnp.broadcast_to(merged[which, pl.ds(row, 1), :], (16, LANES))
                )
                highs.append(joint_high)
                lows.append(joint_low)
            count = lax.broadcasted_iota(jnp.int32, (16, LANES), 0)
            for first in range(0, span, 16):
                key = (count + first).astype(small)
                by_high = jnp.zeros((16, LANES), BF16)
                by_low = jnp.zeros((16, LANES), BF16)
                for which in range(NB):
                    hit = spots[which] == key
                    by_high = jnp.where(hit, highs[which], by_high)
                    by_low = jnp.where(hit, lows[which], by_low)
                matrix[at, first : first + 16, 0:LANES] = by_high
                matrix[at, first : first + 16, LANES : 2 * LANES] = by_low

    spread(levels, total, column, wide, matrix, lanes, codes, coefs, mix)


def prepare(state, coef, offset, vert, wet, low, high):
    levels, cells = state.shape
    rows = cells // LANES
    total = rows + 2 * HALO
    pitch = total + 2 * PAD
    span = (2 * REACH + 1) * LANES
    tiles = total // CHUNK * (CHUNK - 8)
    level_shape = pltpu.VMEM((levels, total, LANES), F32)
    index_shape = pltpu.VMEM((NB, total, LANES), jnp.int32)
    return pl.pallas_call(
        prepare_kernel,
        out_shape=[
            pltpu.VMEM((levels * pitch, LANES), F32),
            pltpu.VMEM((levels * total, LANES), F32),
            pltpu.VMEM((tiles, span, 2 * LANES), BF16),
            level_shape,
            level_shape,
            level_shape,
            index_shape,
            index_shape,
            pltpu.VMEM((NB, total, LANES), F32),
            pltpu.VMEM((total, LANES), F32),
            pltpu.VMEM((total, LANES), F32),
        ],
        in_specs=[pl.BlockSpec(memory_space=pltpu.VMEM)] * 7,
        out_specs=[pl.BlockSpec(memory_space=pltpu.VMEM)] * 11,
        scratch_shapes=[
            pltpu.VMEM((2 * levels, pitch * LANES), BF16),
            pltpu.VMEM((NB, total, LANES), jnp.int32),
            pltpu.VMEM((NB, total, LANES), F32),
            pltpu.VMEM((levels - 1, total, LANES), F32),
        ],
        compiler_params=pltpu.CompilerParams(vmem_limit_bytes=14 * MIB),
        name="prepare",
    )(state, coef, offset, vert, wet, low, high)


def interval_kernel(
    width, column, mix, matrix, inv, from_up, from_down, lanes, codes, coefs, keep, wets,
    imported, low, high,
    state_out, imported_out, first, second, mixed, wide, force, flat,
):
    levels, total = inv.shape[0], inv.shape[1]
    rows = total - 2 * HALO
    pitch = column.shape[0] // levels

    force[:, 0:HALO, :] = low[...]
    force[:, HALO : HALO + rows, :] = imported[...]
    force[:, HALO + rows : total, :] = high[...]
    for field in range(width):
        flat[pl.ds(field * rows, rows), :] = imported[field]

    @pl.loop(0, rows, unroll=8)
    def _(row):
        here = pl.ds(pl.multiple_of(row * LANES, LANES), LANES)
        imported_out[:, here] = flat[pl.ds(row, width, stride=rows), :]

    def solve(source, spread_sum, out):
        @pl.loop(0, total // 8)
        def _(group):
            row = pl.multiple_of(group * 8, 8)
            here = pl.ds(row, 8)
            left = keep[here, :]
            wet = wets[here, :]
            partial = []
            for level in range(levels):
                value = left * source[pl.ds(level * pitch + PAD + row, 8), :]
                value = value + spread_sum[pl.ds(level * total + row, 8), :]
                if level < width:
                    value = value + force[level, here, :] * wet
                value = value * inv[level, here, :]
                if level:
                    value = value + from_up[level, here, :] * partial[-1]
                partial.append(value)
            following = partial[-1]
            out[pl.ds((levels - 1) * pitch + PAD + row, 8), :] = following
            for level in range(levels - 2, -1, -1):
                following = partial[level] + from_down[level, here, :] * following
                out[pl.ds(level * pitch + PAD + row, 8), :] = following

    buffers = (first, second)
    solve(column, mix, first)
    for step in range(1, STEPS):
        source, out = buffers[(step - 1) % 2], buffers[step % 2]
        to_lanes(levels, total, source, wide)
        spread(levels, total, source, wide, matrix, lanes, codes, coefs, mixed)
        solve(source, mixed, out)

    last = buffers[(STEPS - 1) % 2]

    @pl.loop(0, rows, unroll=8)
    def _(row):
        here = pl.ds(pl.multiple_of(row * LANES, LANES), LANES)
        for level in range(0, levels, 8):
            at = level * pitch + PAD + HALO + row
            state_out[level : level + 8, here] = last[pl.ds(at, 8, stride=pitch), :]


def interval(column, mix, matrix, inv, *rest):
    levels, total = inv.shape[0], inv.shape[1]
    pitch = column.shape[0] // levels
    width, rows = rest[-3].shape[0], rest[-3].shape[1]
    operands = (column, mix, matrix, inv, *rest)
    return pl.pallas_call(
        functools.partial(interval_kernel, width),
        out_shape=[
            jax.ShapeDtypeStruct((levels, rows * LANES), F32),
            jax.ShapeDtypeStruct((width, rows * LANES), F32),
        ],
        in_specs=[pl.BlockSpec(memory_space=pltpu.VMEM)] * len(operands),
        out_specs=[pl.BlockSpec(memory_space=pltpu.VMEM)] * 2,
        scratch_shapes=[
            pltpu.VMEM(column.shape, F32),
            pltpu.VMEM(column.shape, F32),
            pltpu.VMEM(mix.shape, F32),
            pltpu.VMEM((2 * levels, pitch * LANES), BF16),
            pltpu.VMEM((width, total, LANES), F32),
            pltpu.VMEM((width * rows, LANES), F32),
        ],
        compiler_params=pltpu.CompilerParams(vmem_limit_bytes=14 * MIB),
        name="interval",
    )(*operands)


def local(
    state,
    export_fields,
    remap_weights,
    routes,
    target_block,
    source_block,
    wet_mask,
    edge_coeff,
    edge_offset,
    vert_coeff,
):
    owners = lax.axis_size("dom")
    comps = lax.axis_size("comp")
    cells = state.shape[2]
    block_count = remap_weights.shape[1]
    capacity = max(2, 2 * block_count // owners)
    width = export_fields.shape[1]
    rows = cells // LANES
    me = lax.axis_index("dom").astype(jnp.int32)[None]
    coef = edge_coeff[0].reshape(-1, rows, LANES)
    offset = edge_offset[0].reshape(-1, rows, LANES)
    vert = vert_coeff[0].reshape(-1, rows, LANES)
    wet = wet_mask.reshape(rows, LANES)

    values, low, high = remap(
        routes[0, :, 0],
        target_block[0],
        source_block[0],
        me,
        export_fields[0],
        remap_weights[0],
        state[0],
        (coef, offset, vert, wet),
        owners,
        capacity,
    )
    values = lax.all_to_all(values, "dom", split_axis=0, concat_axis=0, tiled=True)

    forward = [(i, (i + 1) % owners) for i in range(owners)]
    backward = [(target, source) for source, target in forward]
    low = lax.ppermute(low, "dom", forward)
    high = lax.ppermute(high, "dom", backward)
    prepared = prepare(state[0], coef, offset, vert, wet, low, high)

    pitch = capacity * width + 8
    summed, first_rows, last_rows = assemble(
        values.reshape(owners * pitch, LANES), owners, capacity, width, rows
    )

    def across(value, shift):
        pairs = [
            (comp * owners + dom, (comp + 1) % comps * owners + (dom + shift) % owners)
            for comp in range(comps)
            for dom in range(owners)
        ]
        return lax.ppermute(value, ("comp", "dom"), pairs)

    imported = across(summed, 0)
    from_low = across(last_rows, 1)
    from_high = across(first_rows, -1)
    new_state, imported = interval(*prepared, imported, from_low, from_high)
    return (new_state[None], imported[None])


def solution(mesh):
    placed = (
        P("comp", None, "dom"),
        P("comp", None, "dom"),
        P("comp", "dom", None, None),
        P("comp", "dom", None),
        P("comp", "dom"),
        P("comp", "dom"),
        P("comp", "dom"),
        P("comp", None, "dom"),
        P("comp", None, "dom"),
        P("comp", None, "dom"),
    )
    return jax.shard_map(
        local,
        mesh=mesh,
        in_specs=placed,
        out_specs=(P("comp", None, "dom"), P("comp", None, "dom")),
        check_vma=False,
    )
```

```python
import functools

import jax
import jax.numpy as jnp
from jax import lax
from jax.experimental import pallas as pl
from jax.experimental.pallas import tpu as pltpu
from jax.sharding import PartitionSpec as P

NB = 6
RIM = 256
STEPS = 4
LANES = 128
REACH = RIM // LANES
WINDOW = 2 * REACH + 1
HALO = STEPS * REACH
PAD = 8
MIB = 2**20
CHUNK = 3 * 8

force_scale = 0.5

F32 = jnp.float32
BF16 = jnp.bfloat16


def split(value):
    high = value.astype(BF16)
    return high, (value - high.astype(F32)).astype(BF16)


def remap_kernel(
    owners, capacity, routes, target, source, me, fields, weights, *refs
):
    edges, (out, low, high, counts) = refs[:10], refs[10:]
    step = pl.program_id(0)
    per_step = weights.shape[0]
    width = fields.shape[0]
    lane = lax.broadcasted_iota(jnp.int32, (1, LANES), 1)
    label_row = capacity * width

    @pl.when(step == 0)
    def _():
        out[...] = jnp.zeros_like(out)
        for owner in range(owners):
            counts[owner] = 0
        for side, pack in ((0, low), (1, high)):
            state, coef, offset, vert, wet = edges[side::2]
            levels = state.shape[0]
            for row in range(HALO):
                for level in range(0, levels, 8):
                    tile = state[level : level + 8, row * LANES : (row + 1) * LANES]
                    pack[pl.ds(level * HALO + row, 8, stride=HALO), :] = tile
            at = levels * HALO
            for part in (coef, offset, vert):
                for index in range(part.shape[0]):
                    pack[at : at + HALO, :] = part[index].astype(F32)
                    at += HALO
            pack[at : at + HALO, :] = wet[...].astype(F32)

    for local_block in range(per_step):
        block = step * per_step + local_block
        owner = routes[block]
        rank = counts[owner]
        counts[owner] = rank + 1
        start = pl.multiple_of(source[block] * LANES, LANES)
        picked_high, picked_low = split(fields[:, pl.ds(start, LANES)])
        picked = jnp.concatenate([picked_high, picked_low], axis=0)
        high_part, low_part = split(weights[local_block])
        by_high = jnp.dot(picked, high_part, preferred_element_type=F32)
        by_low = jnp.dot(picked, low_part, preferred_element_type=F32)
        value = (by_low[:width] + by_low[width:] + by_high[width:]) + by_high[:width]
        row = pl.multiple_of(rank * width, width)
        out[owner, pl.ds(row, width), :] = value
        slot = lax.rem(me[0] * capacity + rank, LANES)
        old = out[owner, label_row : label_row + 1, :]
        out[owner, label_row : label_row + 1, :] = jnp.where(
            lane == slot, (target[block] + 1).astype(F32), old
        )


def remap(routes, target, source, me, fields, weights, state, parts, owners, capacity):
    block_count = weights.shape[0]
    width, cells = fields.shape
    levels = state.shape[0]
    rows = cells // LANES
    per_step = 16
    edge = HALO * LANES
    ends = (rows // HALO - 1, 0)
    specs = [pl.BlockSpec((levels, edge), lambda i, *_, e=e: (0, e)) for e in ends]
    edges = [state, state]
    pack_rows = levels * HALO
    for part in parts:
        if part.ndim == 3:
            count = part.shape[0]
            specs += [
                pl.BlockSpec((count, HALO, LANES), lambda i, *_, e=e: (0, e, 0)) for e in ends
            ]
        else:
            count = 1
            specs += [pl.BlockSpec((HALO, LANES), lambda i, *_, e=e: (e, 0)) for e in ends]
        pack_rows += count * HALO
        edges += [part, part]
    slots = (owners, capacity * width + 8, LANES)
    return pl.pallas_call(
        functools.partial(remap_kernel, owners, capacity),
        grid_spec=pltpu.PrefetchScalarGridSpec(
            num_scalar_prefetch=4,
            grid=(block_count // per_step,),
            in_specs=[
                pl.BlockSpec((width, cells), lambda i, *_: (0, 0)),
                pl.BlockSpec((per_step, LANES, LANES), lambda i, *_: (i, 0, 0)),
                *specs,
            ],
            out_specs=[
                pl.BlockSpec(slots, lambda i, *_: (0, 0, 0)),
                pl.BlockSpec((pack_rows, LANES), lambda i, *_: (0, 0)),
                pl.BlockSpec((pack_rows, LANES), lambda i, *_: (0, 0)),
            ],
            scratch_shapes=[pltpu.SMEM((owners,), jnp.int32)],
        ),
        out_shape=[
            jax.ShapeDtypeStruct(slots, F32),
            jax.ShapeDtypeStruct((pack_rows, LANES), F32),
            jax.ShapeDtypeStruct((pack_rows, LANES), F32),
        ],
        compiler_params=pltpu.CompilerParams(vmem_limit_bytes=60 * MIB),
        name="remap",
    )(routes, target, source, me, fields, weights, *edges)


def assemble_kernel(owners, capacity, width, slots, out, low, high, hot, values):
    rows = out.shape[1]
    count = owners * capacity
    per_row = LANES // capacity
    size = capacity * width
    pitch = size + 8
    block = lax.broadcasted_iota(jnp.int32, (rows, LANES), 0) + 1
    for sender in range(owners):
        values[sender * size : (sender + 1) * size, :] = slots[
            sender * pitch : sender * pitch + size, :
        ]
    for half in range(count // LANES):
        label = None
        for sender in range(half * per_row, (half + 1) * per_row):
            row = slots[sender * pitch + size : sender * pitch + size + 1, :]
            label = row if label is None else label + row
        label = jnp.broadcast_to(label.astype(jnp.int32), (rows, LANES))
        hot[:, half * LANES : (half + 1) * LANES] = (label == block).astype(F32).astype(BF16)
    picks = hot[...]
    for field in range(width):
        value_high, value_low = split(values[pl.ds(field, count, stride=width), :])
        both = jnp.concatenate([value_high, value_low], axis=1)
        total = jnp.dot(picks, both, preferred_element_type=F32)
        total = total[:, :LANES] + total[:, LANES:]
        out[field] = total
        low[field] = total[:HALO]
        high[field] = total[rows - HALO :]


def assemble(slots, owners, capacity, width, rows):
    return pl.pallas_call(
        functools.partial(assemble_kernel, owners, capacity, width),
        out_shape=[
            jax.ShapeDtypeStruct((width, rows, LANES), F32),
            jax.ShapeDtypeStruct((width, HALO, LANES), F32),
            jax.ShapeDtypeStruct((width, HALO, LANES), F32),
        ],
        scratch_shapes=[
            pltpu.VMEM((rows, owners * capacity), BF16),
            pltpu.VMEM((owners * capacity * width, LANES), F32),
        ],
        compiler_params=pltpu.CompilerParams(vmem_limit_bytes=12 * MIB),
        name="assemble",
    )(slots)


def lane_pick(value, index):
    return jnp.take_along_axis(value, index, axis=1, mode="promise_in_bounds")


def to_lanes(levels, total, column, wide):
    pitch = column.shape[0] // levels

    @pl.loop(0, total, unroll=8)
    def _(row):
        here = pl.ds(pl.multiple_of((row + PAD) * LANES, LANES), LANES)
        tiles = [
            column[pl.ds(level * pitch + PAD + row, 8, stride=pitch), :]
            for level in range(0, levels, 8)
        ]
        high, low = split(jnp.concatenate(tiles, axis=0))
        wide[0:levels, here] = high
        wide[levels : 2 * levels, here] = low


def spread(levels, total, column, wide, matrix, lanes, codes, coefs, mix):
    pitch = column.shape[0] // levels
    span = WINDOW * LANES

    @pl.loop(0, total // CHUNK)
    def _(chunk):
        base = pl.multiple_of(chunk * CHUNK, 8)
        for tile in range(CHUNK - 8):
            row = base + tile
            at = pl.multiple_of((row + PAD - REACH) * LANES, LANES)
            entry = chunk * (CHUNK - 8) + tile
            got = jnp.dot(
                wide[:, pl.ds(at, span)],
                jnp.concatenate([part[entry] for part in matrix], axis=0),
                preferred_element_type=F32,
            )
            got = got[:, :LANES] + got[:, LANES:]
            got = got[:levels] + got[levels:]
            for level in range(0, levels, 8):
                mix[pl.ds(level * total + row, 8, stride=total), :] = got[level : level + 8]
        row = base + CHUNK - 8
        here = pl.ds(row, 8)
        right = [None] * levels
        for which in range(NB):
            index = lanes[which, here, :]
            code = codes[which, here, :]
            factor = coefs[which, here, :]
            for level in range(levels):
                found = None
                for reach in range(WINDOW):
                    at = level * pitch + PAD - REACH + reach + row
                    picked = lane_pick(column[pl.ds(at, 8), :], index)
                    found = picked if found is None else jnp.where(code == reach, picked, found)
                found = factor * found
                right[level] = found if which == 0 else right[level] + found
        for level in range(levels):
            mix[pl.ds(level * total + row, 8), :] = right[level]


def prepare_kernel(
    state, coef, offset, vert, wet, low, high,
    column, mix, inv, from_up, from_down, lanes, codes, coefs, keep, wets,
    *refs,
):
    matrix, (wide, places, merged, verts) = refs[:WINDOW], refs[WINDOW:]
    levels = state.shape[0]
    rows = state.shape[1] // LANES
    total = rows + 2 * HALO
    pitch = column.shape[0] // levels
    inner = levels - 1

    for pack, first in ((low, 0), (high, total - HALO)):
        for level in range(levels):
            at = level * pitch + PAD + first
            column[at : at + HALO, :] = pack[level * HALO : (level + 1) * HALO, :]
        here = slice(first, first + HALO)
        at = levels * HALO
        for out, count in ((coefs, NB), (places, NB), (verts, inner)):
            for index in range(count):
                out[index, here, :] = pack[at : at + HALO, :].astype(out.dtype)
                at += HALO
        wets[here, :] = pack[at : at + HALO, :] * force_scale
    main = slice(HALO, HALO + rows)
    coefs[:, main, :] = coef[...]
    places[:, main, :] = offset[...]
    verts[:, main, :] = vert[...]
    wets[main, :] = wet[...].astype(F32) * force_scale

    @pl.loop(0, rows, unroll=8)
    def _(row):
        here = pl.ds(pl.multiple_of(row * LANES, LANES), LANES)
        for level in range(0, levels, 8):
            at = level * pitch + PAD + HALO + row
            column[pl.ds(at, 8, stride=pitch), :] = state[level : level + 8, here]

    to_lanes(levels, total, column, wide)
    lane = lax.broadcasted_iota(jnp.int32, (8, LANES), 1)

    @pl.loop(0, total // 8)
    def _(group):
        here = pl.ds(pl.multiple_of(group * 8, 8), 8)
        spots = [places[which, here, :] + lane + RIM for which in range(NB)]
        factors = [coefs[which, here, :] for which in range(NB)]
        left = 1.0
        for which in range(NB):
            places[which, here, :] = spots[which]
            lanes[which, here, :] = jnp.bitwise_and(spots[which], LANES - 1)
            codes[which, here, :] = lax.shift_right_logical(spots[which], 7)
            left = left - factors[which]
            joint = factors[which]
            for other in range(NB):
                if other != which:
                    joint = joint + jnp.where(spots[other] == spots[which], factors[other], 0.0)
            merged[which, here, :] = joint
        keep[here, :] = left
        upper = jnp.zeros((8, LANES), F32)
        carried = jnp.zeros((8, LANES), F32)
        for level in range(levels):
            lower = verts[level, here, :] if level < inner else jnp.zeros((8, LANES), F32)
            pivot = (1.0 + upper + lower) - upper * carried
            inverse = 1.0 / pivot
            carried = lower * inverse
            inv[level, here, :] = inverse
            from_up[level, here, :] = upper * inverse
            from_down[level, here, :] = carried
            upper = lower

    span = WINDOW * LANES
    small = jnp.int16

    @pl.loop(0, total // CHUNK)
    def _(chunk):
        @pl.loop(0, CHUNK - 8)
        def _(tile):
            row = chunk * CHUNK + tile
            at = chunk * (CHUNK - 8) + tile
            spots, highs, lows = [], [], []
            for which in range(NB):
                spot = places[which, pl.ds(row, 1), :]
                spots.append(jnp.broadcast_to(spot, (16, LANES)).astype(small))
                joint_high, joint_low = split(
                    jnp.broadcast_to(merged[which, pl.ds(row, 1), :], (16, LANES))
                )
                highs.append(joint_high)
                lows.append(joint_low)
            count = lax.broadcasted_iota(jnp.int32, (16, LANES), 0)
            for first in range(0, span, 16):
                key = (count + first).astype(small)
                by_high = jnp.zeros((16, LANES), BF16)
                by_low = jnp.zeros((16, LANES), BF16)
                for which in range(NB):
                    hit = spots[which] == key
                    by_high = jnp.where(hit, highs[which], by_high)
                    by_low = jnp.where(hit, lows[which], by_low)
                part, inside = matrix[first // LANES], first % LANES
                part[at, inside : inside + 16, 0:LANES] = by_high
                part[at, inside : inside + 16, LANES : 2 * LANES] = by_low

    spread(levels, total, column, wide, matrix, lanes, codes, coefs, mix)


def prepare(state, coef, offset, vert, wet, low, high):
    levels, cells = state.shape
    rows = cells // LANES
    total = rows + 2 * HALO
    pitch = total + 2 * PAD
    tiles = total // CHUNK * (CHUNK - 8)
    level_shape = pltpu.VMEM((levels, total, LANES), F32)
    index_shape = pltpu.VMEM((NB, total, LANES), jnp.int32)
    return pl.pallas_call(
        prepare_kernel,
        out_shape=[
            pltpu.VMEM((levels * pitch, LANES), F32),
            pltpu.VMEM((levels * total, LANES), F32),
            level_shape,
            level_shape,
            level_shape,
            index_shape,
            index_shape,
            pltpu.VMEM((NB, total, LANES), F32),
            pltpu.VMEM((total, LANES), F32),
            pltpu.VMEM((total, LANES), F32),
            *[pltpu.VMEM((tiles, LANES, 2 * LANES), BF16)] * WINDOW,
        ],
        in_specs=[pl.BlockSpec(memory_space=pltpu.VMEM)] * 7,
        out_specs=[pl.BlockSpec(memory_space=pltpu.VMEM)] * (10 + WINDOW),
        scratch_shapes=[
            pltpu.VMEM((2 * levels, pitch * LANES), BF16),
            pltpu.VMEM((NB, total, LANES), jnp.int32),
            pltpu.VMEM((NB, total, LANES), F32),
            pltpu.VMEM((levels - 1, total, LANES), F32),
        ],
        compiler_params=pltpu.CompilerParams(vmem_limit_bytes=8 * MIB),
        cost_estimate=pl.CostEstimate(
            flops=2 * tiles * 8 * levels * WINDOW * LANES * LANES,
            bytes_accessed=80 * MIB,
            transcendentals=0,
        ),
        name="prepare",
    )(state, coef, offset, vert, wet, low, high)


def interval_kernel(
    width, column, mix, inv, from_up, from_down, lanes, codes, coefs, keep, wets, *refs
):
    matrix, refs = refs[:WINDOW], refs[WINDOW:]
    imported, low, high, state_out, imported_out, first, second, mixed, wide, force, flat = refs
    levels, total = inv.shape[0], inv.shape[1]
    rows = total - 2 * HALO
    pitch = column.shape[0] // levels

    force[:, 0:HALO, :] = low[...]
    force[:, HALO : HALO + rows, :] = imported[...]
    force[:, HALO + rows : total, :] = high[...]
    for field in range(width):
        flat[pl.ds(field * rows, rows), :] = imported[field]

    @pl.loop(0, rows, unroll=8)
    def _(row):
        here = pl.ds(pl.multiple_of(row * LANES, LANES), LANES)
        imported_out[:, here] = flat[pl.ds(row, width, stride=rows), :]

    def solve(source, spread_sum, out):
        @pl.loop(0, total // 8)
        def _(group):
            row = pl.multiple_of(group * 8, 8)
            here = pl.ds(row, 8)
            left = keep[here, :]
            wet = wets[here, :]
            partial = []
            for level in range(levels):
                value = left * source[pl.ds(level * pitch + PAD + row, 8), :]
                value = value + spread_sum[pl.ds(level * total + row, 8), :]
                if level < width:
                    value = value + force[level, here, :] * wet
                value = value * inv[level, here, :]
                if level:
                    value = value + from_up[level, here, :] * partial[-1]
                partial.append(value)
            following = partial[-1]
            out[pl.ds((levels - 1) * pitch + PAD + row, 8), :] = following
            for level in range(levels - 2, -1, -1):
                following = partial[level] + from_down[level, here, :] * following
                out[pl.ds(level * pitch + PAD + row, 8), :] = following

    buffers = (first, second)
    solve(column, mix, first)
    for step in range(1, STEPS):
        source, out = buffers[(step - 1) % 2], buffers[step % 2]
        to_lanes(levels, total, source, wide)
        spread(levels, total, source, wide, matrix, lanes, codes, coefs, mixed)
        solve(source, mixed, out)

    last = buffers[(STEPS - 1) % 2]

    @pl.loop(0, rows, unroll=8)
    def _(row):
        here = pl.ds(pl.multiple_of(row * LANES, LANES), LANES)
        for level in range(0, levels, 8):
            at = level * pitch + PAD + HALO + row
            state_out[level : level + 8, here] = last[pl.ds(at, 8, stride=pitch), :]


def interval(column, mix, inv, *rest):
    levels, total = inv.shape[0], inv.shape[1]
    pitch = column.shape[0] // levels
    width, rows = rest[-3].shape[0], rest[-3].shape[1]
    operands = (column, mix, inv, *rest)
    return pl.pallas_call(
        functools.partial(interval_kernel, width),
        out_shape=[
            jax.ShapeDtypeStruct((levels, rows * LANES), F32),
            jax.ShapeDtypeStruct((width, rows * LANES), F32),
        ],
        in_specs=[pl.BlockSpec(memory_space=pltpu.VMEM)] * len(operands),
        out_specs=[pl.BlockSpec(memory_space=pltpu.VMEM)] * 2,
        scratch_shapes=[
            pltpu.VMEM(column.shape, F32),
            pltpu.VMEM(column.shape, F32),
            pltpu.VMEM(mix.shape, F32),
            pltpu.VMEM((2 * levels, pitch * LANES), BF16),
            pltpu.VMEM((width, total, LANES), F32),
            pltpu.VMEM((width * rows, LANES), F32),
        ],
        compiler_params=pltpu.CompilerParams(vmem_limit_bytes=10 * MIB),
        name="interval",
    )(*operands)


def local(
    state,
    export_fields,
    remap_weights,
    routes,
    target_block,
    source_block,
    wet_mask,
    edge_coeff,
    edge_offset,
    vert_coeff,
):
    owners = lax.axis_size("dom")
    comps = lax.axis_size("comp")
    cells = state.shape[2]
    block_count = remap_weights.shape[1]
    capacity = max(2, 2 * block_count // owners)
    width = export_fields.shape[1]
    rows = cells // LANES
    me = lax.axis_index("dom").astype(jnp.int32)[None]
    coef = edge_coeff[0].reshape(-1, rows, LANES)
    offset = edge_offset[0].reshape(-1, rows, LANES)
    vert = vert_coeff[0].reshape(-1, rows, LANES)
    wet = wet_mask.reshape(rows, LANES)

    values, low, high = remap(
        routes[0, :, 0],
        target_block[0],
        source_block[0],
        me,
        export_fields[0],
        remap_weights[0],
        state[0],
        (coef, offset, vert, wet),
        owners,
        capacity,
    )
    values = lax.all_to_all(values, "dom", split_axis=0, concat_axis=0, tiled=True)

    forward = [(i, (i + 1) % owners) for i in range(owners)]
    backward = [(target, source) for source, target in forward]
    low = lax.ppermute(low, "dom", forward)
    high = lax.ppermute(high, "dom", backward)
    prepared = prepare(state[0], coef, offset, vert, wet, low, high)
    values, prepared = lax.optimization_barrier((values, prepared))

    pitch = capacity * width + 8
    summed, first_rows, last_rows = assemble(
        values.reshape(owners * pitch, LANES), owners, capacity, width, rows
    )

    def across(value, shift):
        pairs = [
            (comp * owners + dom, (comp + 1) % comps * owners + (dom + shift) % owners)
            for comp in range(comps)
            for dom in range(owners)
        ]
        return lax.ppermute(value, ("comp", "dom"), pairs)

    imported = across(summed, 0)
    from_low = across(last_rows, 1)
    from_high = across(first_rows, -1)
    new_state, imported = interval(*prepared, imported, from_low, from_high)
    return (new_state[None], imported[None])


def solution(mesh):
    placed = (
        P("comp", None, "dom"),
        P("comp", None, "dom"),
        P("comp", "dom", None, None),
        P("comp", "dom", None),
        P("comp", "dom"),
        P("comp", "dom"),
        P("comp", "dom"),
        P("comp", None, "dom"),
        P("comp", None, "dom"),
        P("comp", None, "dom"),
    )
    return jax.shard_map(
        local,
        mesh=mesh,
        in_specs=placed,
        out_specs=(P("comp", None, "dom"), P("comp", None, "dom")),
        check_vma=False,
    )
```

```python
import functools

import jax
import jax.numpy as jnp
from jax import lax
from jax.experimental import pallas as pl
from jax.experimental.pallas import tpu as pltpu
from jax.sharding import PartitionSpec as P

NB = 6
RIM = 256
STEPS = 4
LANES = 128
REACH = RIM // LANES
WINDOW = 2 * REACH + 1
HALO = STEPS * REACH
PAD = 8
MIB = 2**20
GROUP = 8
CHUNK = 2 * GROUP

force_scale = 0.5

F32 = jnp.float32
BF16 = jnp.bfloat16


def split(value):
    high = value.astype(BF16)
    return high, (value - high.astype(F32)).astype(BF16)


def remap_kernel(
    owners, capacity, routes, target, source, me, fields, weights, *refs
):
    edges, (out, low, high, counts) = refs[:10], refs[10:]
    step = pl.program_id(0)
    per_step = weights.shape[0]
    width = fields.shape[0]
    lane = lax.broadcasted_iota(jnp.int32, (1, LANES), 1)
    label_row = capacity * width

    @pl.when(step == 0)
    def _():
        out[...] = jnp.zeros_like(out)
        for owner in range(owners):
            counts[owner] = 0
        for side, pack in ((0, low), (1, high)):
            state, coef, offset, vert, wet = edges[side::2]
            levels = state.shape[0]
            for row in range(HALO):
                for level in range(0, levels, 8):
                    tile = state[level : level + 8, row * LANES : (row + 1) * LANES]
                    pack[pl.ds(level * HALO + row, 8, stride=HALO), :] = tile
            at = levels * HALO
            for part in (coef, offset, vert):
                for index in range(part.shape[0]):
                    pack[at : at + HALO, :] = part[index].astype(F32)
                    at += HALO
            pack[at : at + HALO, :] = wet[...].astype(F32)

    for local_block in range(per_step):
        block = step * per_step + local_block
        owner = routes[block]
        rank = counts[owner]
        counts[owner] = rank + 1
        start = pl.multiple_of(source[block] * LANES, LANES)
        picked_high, picked_low = split(fields[:, pl.ds(start, LANES)])
        picked = jnp.concatenate([picked_high, picked_low], axis=0)
        high_part, low_part = split(weights[local_block])
        by_high = jnp.dot(picked, high_part, preferred_element_type=F32)
        by_low = jnp.dot(picked, low_part, preferred_element_type=F32)
        value = (by_low[:width] + by_low[width:] + by_high[width:]) + by_high[:width]
        row = pl.multiple_of(rank * width, width)
        out[owner, pl.ds(row, width), :] = value
        slot = lax.rem(me[0] * capacity + rank, LANES)
        old = out[owner, label_row : label_row + 1, :]
        out[owner, label_row : label_row + 1, :] = jnp.where(
            lane == slot, (target[block] + 1).astype(F32), old
        )


def remap(routes, target, source, me, fields, weights, state, parts, owners, capacity):
    block_count = weights.shape[0]
    width, cells = fields.shape
    levels = state.shape[0]
    rows = cells // LANES
    per_step = 16
    edge = HALO * LANES
    ends = (rows // HALO - 1, 0)
    specs = [pl.BlockSpec((levels, edge), lambda i, *_, e=e: (0, e)) for e in ends]
    edges = [state, state]
    pack_rows = levels * HALO
    for part in parts:
        if part.ndim == 3:
            count = part.shape[0]
            specs += [
                pl.BlockSpec((count, HALO, LANES), lambda i, *_, e=e: (0, e, 0)) for e in ends
            ]
        else:
            count = 1
            specs += [pl.BlockSpec((HALO, LANES), lambda i, *_, e=e: (e, 0)) for e in ends]
        pack_rows += count * HALO
        edges += [part, part]
    slots = (owners, capacity * width + 8, LANES)
    return pl.pallas_call(
        functools.partial(remap_kernel, owners, capacity),
        grid_spec=pltpu.PrefetchScalarGridSpec(
            num_scalar_prefetch=4,
            grid=(block_count // per_step,),
            in_specs=[
                pl.BlockSpec((width, cells), lambda i, *_: (0, 0)),
                pl.BlockSpec((per_step, LANES, LANES), lambda i, *_: (i, 0, 0)),
                *specs,
            ],
            out_specs=[
                pl.BlockSpec(slots, lambda i, *_: (0, 0, 0)),
                pl.BlockSpec((pack_rows, LANES), lambda i, *_: (0, 0)),
                pl.BlockSpec((pack_rows, LANES), lambda i, *_: (0, 0)),
            ],
            scratch_shapes=[pltpu.SMEM((owners,), jnp.int32)],
        ),
        out_shape=[
            jax.ShapeDtypeStruct(slots, F32),
            jax.ShapeDtypeStruct((pack_rows, LANES), F32),
            jax.ShapeDtypeStruct((pack_rows, LANES), F32),
        ],
        compiler_params=pltpu.CompilerParams(vmem_limit_bytes=60 * MIB),
        name="remap",
    )(routes, target, source, me, fields, weights, *edges)


def assemble_kernel(owners, capacity, width, slots, out, low, high, hot, values):
    rows = out.shape[1]
    count = owners * capacity
    per_row = LANES // capacity
    size = capacity * width
    pitch = size + 8
    block = lax.broadcasted_iota(jnp.int32, (rows, LANES), 0) + 1
    for sender in range(owners):
        values[sender * size : (sender + 1) * size, :] = slots[
            sender * pitch : sender * pitch + size, :
        ]
    for half in range(count // LANES):
        label = None
        for sender in range(half * per_row, (half + 1) * per_row):
            row = slots[sender * pitch + size : sender * pitch + size + 1, :]
            label = row if label is None else label + row
        label = jnp.broadcast_to(label.astype(jnp.int32), (rows, LANES))
        hot[:, half * LANES : (half + 1) * LANES] = (label == block).astype(F32).astype(BF16)
    picks = hot[...]
    for field in range(width):
        value_high, value_low = split(values[pl.ds(field, count, stride=width), :])
        both = jnp.concatenate([value_high, value_low], axis=1)
        total = jnp.dot(picks, both, preferred_element_type=F32)
        total = total[:, :LANES] + total[:, LANES:]
        out[field] = total
        low[field] = total[:HALO]
        high[field] = total[rows - HALO :]


def assemble(slots, owners, capacity, width, rows):
    return pl.pallas_call(
        functools.partial(assemble_kernel, owners, capacity, width),
        out_shape=[
            jax.ShapeDtypeStruct((width, rows, LANES), F32),
            jax.ShapeDtypeStruct((width, HALO, LANES), F32),
            jax.ShapeDtypeStruct((width, HALO, LANES), F32),
        ],
        scratch_shapes=[
            pltpu.VMEM((rows, owners * capacity), BF16),
            pltpu.VMEM((owners * capacity * width, LANES), F32),
        ],
        compiler_params=pltpu.CompilerParams(vmem_limit_bytes=12 * MIB),
        name="assemble",
    )(slots)


def lane_pick(value, index):
    return jnp.take_along_axis(value, index, axis=1, mode="promise_in_bounds")


def group_rows(chunk, chunks):
    base = chunk * CHUNK
    late = (chunk > chunks // 2).astype(jnp.int32) * GROUP
    return pl.multiple_of(base + GROUP - late, GROUP), pl.multiple_of(base + late, GROUP)


def to_lanes(levels, column, wide, row):
    pitch = column.shape[0] // levels
    here = pl.ds(pl.multiple_of((row + PAD) * LANES, LANES), LANES)
    tiles = [
        column[pl.ds(level * pitch + PAD + row, 8, stride=pitch), :]
        for level in range(0, levels, 8)
    ]
    high, low = split(jnp.concatenate(tiles, axis=0))
    wide[0:levels, here] = high
    wide[levels : 2 * levels, here] = low


def spread_tile(levels, total, wide, matrix, entry, row, mix):
    at = pl.multiple_of((row + PAD - REACH) * LANES, LANES)
    got = jnp.dot(
        wide[:, pl.ds(at, WINDOW * LANES)],
        jnp.concatenate([part[entry] for part in matrix], axis=0),
        preferred_element_type=F32,
    )
    got = got[:, :LANES] + got[:, LANES:]
    got = got[:levels] + got[levels:]
    for level in range(0, levels, 8):
        mix[pl.ds(level * total + row, 8, stride=total), :] = got[level : level + 8]


def spread_group(levels, total, column, row, terms, mix):
    pitch = column.shape[0] // levels
    right = [None] * levels
    for which in range(NB):
        index, code, factor = terms(which)
        for level in range(levels):
            found = None
            for reach in range(WINDOW):
                at = level * pitch + PAD - REACH + reach + row
                picked = lane_pick(column[pl.ds(at, GROUP), :], index)
                found = picked if found is None else jnp.where(code == reach, picked, found)
            found = factor * found
            right[level] = found if which == 0 else right[level] + found
    for level in range(levels):
        mix[pl.ds(level * total + row, GROUP), :] = right[level]


def spots_of(offset):
    return offset + lax.broadcasted_iota(jnp.int32, offset.shape, offset.ndim - 1) + RIM


def lane_of(spot):
    return jnp.bitwise_and(spot, LANES - 1)


def code_of(spot):
    return lax.shift_right_logical(spot, LANES.bit_length() - 1)


def state_rows(state, column, row):
    levels = state.shape[0]
    pitch = column.shape[0] // levels
    here = pl.ds(pl.multiple_of(row * LANES, LANES), LANES)
    for level in range(0, levels, 8):
        at = level * pitch + PAD + HALO + row
        column[pl.ds(at, 8, stride=pitch), :] = state[level : level + 8, here]


def build_kernel(state, coef, offset, matrix, mix, column, wide, spots, highs, lows):
    chunk = pl.program_id(0)
    chunks = pl.num_programs(0)
    levels = state.shape[0]
    rows = state.shape[1] // LANES
    total = rows + 2 * HALO

    @pl.when(chunk == 0)
    def _():
        @pl.loop(0, rows, unroll=8)
        def _(row):
            state_rows(state, column, row)

        @pl.loop(0, rows, unroll=8)
        def _(row):
            to_lanes(levels, column, wide, row + HALO)

    by_matrix, by_gather = group_rows(chunk, chunks)
    here = pl.ds(pl.multiple_of(by_matrix - HALO, GROUP), GROUP)
    spot = [spots_of(offset[which, here, :]) for which in range(NB)]
    factor = [coef[which, here, :] for which in range(NB)]
    for which in range(NB):
        spots[which] = spot[which]
        joint = factor[which]
        for other in range(NB):
            if other != which:
                joint = joint + jnp.where(spot[other] == spot[which], factor[other], 0.0)
        high = joint.astype(BF16).astype(F32)
        highs[which] = high
        lows[which] = joint - high

    small = jnp.int16

    @pl.loop(0, GROUP, unroll=8)
    def _(tile):
        def wide_row(ref, kind):
            return [
                jnp.broadcast_to(ref[which, pl.ds(tile, 1), :], (16, LANES)).astype(kind)
                for which in range(NB)
            ]

        spot_rows, high_rows, low_rows = (
            wide_row(spots, small),
            wide_row(highs, BF16),
            wide_row(lows, BF16),
        )
        count = lax.broadcasted_iota(jnp.int32, (16, LANES), 0).astype(small)
        for first in range(0, WINDOW * LANES, 16):
            key = count + small(first)
            by_high = jnp.zeros((16, LANES), BF16)
            by_low = jnp.zeros((16, LANES), BF16)
            for which in range(NB):
                hit = spot_rows[which] == key
                by_high = jnp.where(hit, high_rows[which], by_high)
                by_low = jnp.where(hit, low_rows[which], by_low)
            matrix[tile, first : first + 16, 0:LANES] = by_high
            matrix[tile, first : first + 16, LANES : 2 * LANES] = by_low

    for tile in range(GROUP):
        parts = [matrix.at[:, pl.ds(reach * LANES, LANES), :] for reach in range(WINDOW)]
        spread_tile(levels, total, wide, parts, tile, by_matrix + tile, mix)

    @pl.when((chunk > 0) & (chunk < chunks - 1))
    def _():
        near = pl.ds(pl.multiple_of(by_gather - HALO, GROUP), GROUP)

        def terms(which):
            spot = spots_of(offset[which, near, :])
            return lane_of(spot), code_of(spot), coef[which, near, :]

        spread_group(levels, total, column, by_gather, terms, mix)


def build(state, coef, offset):
    levels, cells = state.shape
    rows = cells // LANES
    total = rows + 2 * HALO
    pitch = total + 2 * PAD
    chunks = total // CHUNK
    span = WINDOW * LANES
    return pl.pallas_call(
        build_kernel,
        grid=(chunks,),
        in_specs=[
            pl.BlockSpec(state.shape, lambda i: (0, 0)),
            pl.BlockSpec(coef.shape, lambda i: (0, 0, 0)),
            pl.BlockSpec(offset.shape, lambda i: (0, 0, 0)),
        ],
        out_specs=[
            pl.BlockSpec((GROUP, span, 2 * LANES), lambda i: (i, 0, 0)),
            pl.BlockSpec((levels * total, LANES), lambda i: (0, 0)),
        ],
        out_shape=[
            jax.ShapeDtypeStruct((chunks * GROUP, span, 2 * LANES), BF16),
            jax.ShapeDtypeStruct((levels * total, LANES), F32),
        ],
        scratch_shapes=[
            pltpu.VMEM((levels * pitch, LANES), F32),
            pltpu.VMEM((2 * levels, pitch * LANES), BF16),
            pltpu.VMEM((NB, GROUP, LANES), jnp.int32),
            pltpu.VMEM((NB, GROUP, LANES), F32),
            pltpu.VMEM((NB, GROUP, LANES), F32),
        ],
        compiler_params=pltpu.CompilerParams(vmem_limit_bytes=56 * MIB),
        cost_estimate=pl.CostEstimate(
            flops=2 * chunks * GROUP * 2 * levels * span * 2 * LANES,
            bytes_accessed=80 * MIB,
            transcendentals=0,
        ),
        name="build",
    )(state, coef, offset)


def prepare_kernel(
    state, coef, offset, vert, wet, low, high, matrix_far, mix_far,
    column, mix, inv, from_up, from_down, lanes, codes, coefs, keep, wets, *refs
):
    matrix, (verts, copied, mixed) = refs[:WINDOW], refs[WINDOW:]
    levels = state.shape[0]
    rows = state.shape[1] // LANES
    total = rows + 2 * HALO
    pitch = column.shape[0] // levels
    inner = levels - 1

    mix_copy = pltpu.make_async_copy(mix_far, mix, mixed)
    mix_copy.start()
    matrix_copies = [
        pltpu.make_async_copy(
            matrix_far.at[:, pl.ds(reach * LANES, LANES), :], matrix[reach], copied.at[reach]
        )
        for reach in range(WINDOW)
    ]
    for copy in matrix_copies:
        copy.start()

    for pack, first in ((low, 0), (high, total - HALO)):
        for level in range(levels):
            at = level * pitch + PAD + first
            column[at : at + HALO, :] = pack[level * HALO : (level + 1) * HALO, :]
        here = slice(first, first + HALO)
        at = levels * HALO
        for out, count in ((coefs, NB), (lanes, NB), (verts, inner)):
            for index in range(count):
                out[index, here, :] = pack[at : at + HALO, :].astype(out.dtype)
                at += HALO
        wets[here, :] = pack[at : at + HALO, :] * force_scale
    main = slice(HALO, HALO + rows)
    coefs[:, main, :] = coef[...]
    lanes[:, main, :] = offset[...]
    verts[:, main, :] = vert[...]
    wets[main, :] = wet[...].astype(F32) * force_scale

    @pl.loop(0, rows, unroll=8)
    def _(row):
        state_rows(state, column, row)

    @pl.loop(0, total // GROUP)
    def _(group):
        here = pl.ds(pl.multiple_of(group * GROUP, GROUP), GROUP)
        left = 1.0
        for which in range(NB):
            spot = spots_of(lanes[which, here, :])
            lanes[which, here, :] = lane_of(spot)
            codes[which, here, :] = code_of(spot)
            left = left - coefs[which, here, :]
        keep[here, :] = left
        upper = jnp.zeros((GROUP, LANES), F32)
        carried = jnp.zeros((GROUP, LANES), F32)
        for level in range(levels):
            lower = verts[level, here, :] if level < inner else jnp.zeros((GROUP, LANES), F32)
            pivot = (1.0 + upper + lower) - upper * carried
            inverse = 1.0 / pivot
            carried = lower * inverse
            inv[level, here, :] = inverse
            from_up[level, here, :] = upper * inverse
            from_down[level, here, :] = carried
            upper = lower

    mix_copy.wait()

    @pl.loop(0, 4)
    def _(which_group):
        far = (which_group >= 2).astype(jnp.int32)
        row = pl.multiple_of(which_group * GROUP + far * (total - 4 * GROUP), GROUP)
        here = pl.ds(row, GROUP)

        def terms(which):
            return lanes[which, here, :], codes[which, here, :], coefs[which, here, :]

        spread_group(levels, total, column, row, terms, mix)

    for copy in matrix_copies:
        copy.wait()


def prepare(state, coef, offset, vert, wet, low, high, matrix, mix):
    levels, cells = state.shape
    rows = cells // LANES
    total = rows + 2 * HALO
    pitch = total + 2 * PAD
    level_shape = pltpu.VMEM((levels, total, LANES), F32)
    index_shape = pltpu.VMEM((NB, total, LANES), jnp.int32)
    near = pl.BlockSpec(memory_space=pltpu.VMEM)
    far = pl.BlockSpec(memory_space=pltpu.HBM)
    return pl.pallas_call(
        prepare_kernel,
        out_shape=[
            pltpu.VMEM((levels * pitch, LANES), F32),
            pltpu.VMEM(mix.shape, F32),
            level_shape,
            level_shape,
            level_shape,
            index_shape,
            index_shape,
            pltpu.VMEM((NB, total, LANES), F32),
            pltpu.VMEM((total, LANES), F32),
            pltpu.VMEM((total, LANES), F32),
            *[pltpu.VMEM((matrix.shape[0], LANES, 2 * LANES), BF16)] * WINDOW,
        ],
        in_specs=[near] * 7 + [far] * 2,
        out_specs=[near] * (10 + WINDOW),
        scratch_shapes=[
            pltpu.VMEM((levels - 1, total, LANES), F32),
            pltpu.SemaphoreType.DMA((WINDOW,)),
            pltpu.SemaphoreType.DMA,
        ],
        compiler_params=pltpu.CompilerParams(vmem_limit_bytes=12 * MIB),
        cost_estimate=pl.CostEstimate(
            flops=0, bytes_accessed=40 * MIB, transcendentals=0
        ),
        name="prepare",
    )(state, coef, offset, vert, wet, low, high, matrix, mix)


def interval_kernel(
    width, column, mix, inv, from_up, from_down, lanes, codes, coefs, keep, wets, *refs
):
    matrix, refs = refs[:WINDOW], refs[WINDOW:]
    imported, low, high, state_out, imported_out, *refs = refs
    cells, mixed, wide, force, flat = refs
    levels, total = inv.shape[0], inv.shape[1]
    rows = total - 2 * HALO
    pitch = column.shape[0] // levels
    chunks = total // CHUNK

    force[:, 0:HALO, :] = low[...]
    force[:, HALO : HALO + rows, :] = imported[...]
    force[:, HALO + rows : total, :] = high[...]
    for field in range(width):
        flat[pl.ds(field * rows, rows), :] = imported[field]

    @pl.loop(0, rows, unroll=8)
    def _(row):
        here = pl.ds(pl.multiple_of(row * LANES, LANES), LANES)
        imported_out[:, here] = flat[pl.ds(row, width, stride=rows), :]

    def solve(chunk, source, spread_sum, out, wide):
        for group in range(CHUNK // GROUP):
            row = pl.multiple_of(chunk * CHUNK + group * GROUP, GROUP)
            here = pl.ds(row, GROUP)
            left = keep[here, :]
            wet = wets[here, :]
            partial = []
            for level in range(levels):
                value = left * source[pl.ds(level * pitch + PAD + row, GROUP), :]
                value = value + spread_sum[pl.ds(level * total + row, GROUP), :]
                if level < width:
                    value = value + force[level, here, :] * wet
                value = value * inv[level, here, :]
                if level:
                    value = value + from_up[level, here, :] * partial[-1]
                partial.append(value)
            following = partial[-1]
            out[pl.ds((levels - 1) * pitch + PAD + row, GROUP), :] = following
            for level in range(levels - 2, -1, -1):
                following = partial[level] + from_down[level, here, :] * following
                out[pl.ds(level * pitch + PAD + row, GROUP), :] = following
        for row in range(CHUNK):
            to_lanes(levels, out, wide, chunk * CHUNK + row)

    def spread(chunk, source, wide):
        by_matrix, by_gather = group_rows(chunk, chunks)
        for tile in range(GROUP):
            spread_tile(
                levels, total, wide, matrix, chunk * GROUP + tile, by_matrix + tile, mixed
            )
        here = pl.ds(by_gather, GROUP)

        def terms(which):
            return lanes[which, here, :], codes[which, here, :], coefs[which, here, :]

        spread_group(levels, total, source, by_gather, terms, mixed)

    @pl.loop(0, chunks)
    def _(chunk):
        solve(chunk, column, mix, cells, wide)

    @pl.loop(1, STEPS)
    def _(step):
        for chunk in range(chunks):
            spread(jnp.int32(chunk), cells, wide)
        for chunk in range(chunks):
            solve(chunk, cells, mixed, cells, wide)

    @pl.loop(0, rows, unroll=8)
    def _(row):
        here = pl.ds(pl.multiple_of(row * LANES, LANES), LANES)
        for level in range(0, levels, 8):
            at = level * pitch + PAD + HALO + row
            state_out[level : level + 8, here] = cells[pl.ds(at, 8, stride=pitch), :]


def interval(column, mix, inv, *rest):
    levels, total = inv.shape[0], inv.shape[1]
    pitch = column.shape[0] // levels
    width, rows = rest[-3].shape[0], rest[-3].shape[1]
    operands = (column, mix, inv, *rest)
    return pl.pallas_call(
        functools.partial(interval_kernel, width),
        out_shape=[
            jax.ShapeDtypeStruct((levels, rows * LANES), F32),
            jax.ShapeDtypeStruct((width, rows * LANES), F32),
        ],
        in_specs=[pl.BlockSpec(memory_space=pltpu.VMEM)] * len(operands),
        out_specs=[pl.BlockSpec(memory_space=pltpu.VMEM)] * 2,
        scratch_shapes=[
            pltpu.VMEM(column.shape, F32),
            pltpu.VMEM(mix.shape, F32),
            pltpu.VMEM((2 * levels, pitch * LANES), BF16),
            pltpu.VMEM((width, total, LANES), F32),
            pltpu.VMEM((width * rows, LANES), F32),
        ],
        compiler_params=pltpu.CompilerParams(vmem_limit_bytes=12 * MIB),
        name="interval",
    )(*operands)


def local(
    state,
    export_fields,
    remap_weights,
    routes,
    target_block,
    source_block,
    wet_mask,
    edge_coeff,
    edge_offset,
    vert_coeff,
):
    owners = lax.axis_size("dom")
    comps = lax.axis_size("comp")
    cells = state.shape[2]
    block_count = remap_weights.shape[1]
    capacity = max(2, 2 * block_count // owners)
    width = export_fields.shape[1]
    rows = cells // LANES
    me = lax.axis_index("dom").astype(jnp.int32)[None]
    coef = edge_coeff[0].reshape(-1, rows, LANES)
    offset = edge_offset[0].reshape(-1, rows, LANES)
    vert = vert_coeff[0].reshape(-1, rows, LANES)
    wet = wet_mask.reshape(rows, LANES)

    values, low, high = remap(
        routes[0, :, 0],
        target_block[0],
        source_block[0],
        me,
        export_fields[0],
        remap_weights[0],
        state[0],
        (coef, offset, vert, wet),
        owners,
        capacity,
    )
    values = lax.all_to_all(values, "dom", split_axis=0, concat_axis=0, tiled=True)

    forward = [(i, (i + 1) % owners) for i in range(owners)]
    backward = [(target, source) for source, target in forward]
    low = lax.ppermute(low, "dom", forward)
    high = lax.ppermute(high, "dom", backward)
    matrix, mix = build(state[0], coef, offset)
    values, matrix, mix, low, high = lax.optimization_barrier((values, matrix, mix, low, high))

    pitch = capacity * width + 8
    summed, first_rows, last_rows = assemble(
        values.reshape(owners * pitch, LANES), owners, capacity, width, rows
    )

    def across(value, shift):
        pairs = [
            (comp * owners + dom, (comp + 1) % comps * owners + (dom + shift) % owners)
            for comp in range(comps)
            for dom in range(owners)
        ]
        return lax.ppermute(value, ("comp", "dom"), pairs)

    imported = across(summed, 0)
    from_low = across(last_rows, 1)
    from_high = across(first_rows, -1)
    prepared = prepare(state[0], coef, offset, vert, wet, low, high, matrix, mix)
    new_state, imported = interval(*prepared, imported, from_low, from_high)
    return (new_state[None], imported[None])


def solution(mesh):
    placed = (
        P("comp", None, "dom"),
        P("comp", None, "dom"),
        P("comp", "dom", None, None),
        P("comp", "dom", None),
        P("comp", "dom"),
        P("comp", "dom"),
        P("comp", "dom"),
        P("comp", None, "dom"),
        P("comp", None, "dom"),
        P("comp", None, "dom"),
    )
    return jax.shard_map(
        local,
        mesh=mesh,
        in_specs=placed,
        out_specs=(P("comp", None, "dom"), P("comp", None, "dom")),
        check_vma=False,
    )
```

```python
import functools

import jax
import jax.numpy as jnp
from jax import lax
from jax.experimental import pallas as pl
from jax.experimental.pallas import tpu as pltpu
from jax.sharding import PartitionSpec as P

NB = 6
RIM = 256
STEPS = 4
LANES = 128
REACH = RIM // LANES
WINDOW = 2 * REACH + 1
HALO = STEPS * REACH
PAD = 8
MIB = 2**20
GROUP = 8
CHUNK = 2 * GROUP

force_scale = 0.5

F32 = jnp.float32
BF16 = jnp.bfloat16


def split(value):
    high = value.astype(BF16)
    return high, (value - high.astype(F32)).astype(BF16)


def remap_kernel(
    owners, capacity, routes, target, source, me, fields, weights, *refs
):
    edges, (out, low, high, counts, marks) = refs[:10], refs[10:]
    step = pl.program_id(0)
    per_step = weights.shape[0]
    width = fields.shape[0]
    lane = lax.broadcasted_iota(jnp.int32, (1, LANES), 1)
    label_row = capacity * width

    @pl.when(step == 0)
    def _():
        out[...] = jnp.zeros_like(out)
        marks[...] = jnp.zeros_like(marks)
        for owner in range(owners):
            counts[owner] = 0
        for side, pack in ((0, low), (1, high)):
            state, coef, offset, vert, wet = edges[side::2]
            levels = state.shape[0]
            for row in range(HALO):
                for level in range(0, levels, 8):
                    tile = state[level : level + 8, row * LANES : (row + 1) * LANES]
                    pack[pl.ds(level * HALO + row, 8, stride=HALO), :] = tile
            at = levels * HALO
            for part in (coef, offset, vert):
                for index in range(part.shape[0]):
                    pack[at : at + HALO, :] = part[index].astype(F32)
                    at += HALO
            pack[at : at + HALO, :] = wet[...].astype(F32)

    for local_block in range(per_step):
        block = step * per_step + local_block
        owner = routes[block]
        rank = counts[owner]
        counts[owner] = rank + 1
        start = pl.multiple_of(source[block] * LANES, LANES)
        picked_high, picked_low = split(fields[:, pl.ds(start, LANES)])
        picked = jnp.concatenate([picked_high, picked_low], axis=0)
        both = jnp.concatenate(split(weights[local_block]), axis=1)
        product = jnp.dot(picked, both, preferred_element_type=F32)
        product = product[:, :LANES] + product[:, LANES:]
        value = product[:width] + product[width:]
        row = pl.multiple_of(rank * width, width)
        out[owner, pl.ds(row, width), :] = value
        slot = lax.rem(me[0] * capacity + rank, LANES)
        marks[pl.ds(owner, 1), :] = jnp.where(
            lane == slot, (target[block] + 1).astype(F32), marks[pl.ds(owner, 1), :]
        )

    @pl.when(step == pl.num_programs(0) - 1)
    def _():
        for owner in range(owners):
            out[owner, label_row : label_row + 1, :] = marks[owner : owner + 1, :]


def remap(routes, target, source, me, fields, weights, state, parts, owners, capacity):
    block_count = weights.shape[0]
    width, cells = fields.shape
    levels = state.shape[0]
    rows = cells // LANES
    per_step = 16
    edge = HALO * LANES
    ends = (rows // HALO - 1, 0)
    specs = [pl.BlockSpec((levels, edge), lambda i, *_, e=e: (0, e)) for e in ends]
    edges = [state, state]
    pack_rows = levels * HALO
    for part in parts:
        if part.ndim == 3:
            count = part.shape[0]
            specs += [
                pl.BlockSpec((count, HALO, LANES), lambda i, *_, e=e: (0, e, 0)) for e in ends
            ]
        else:
            count = 1
            specs += [pl.BlockSpec((HALO, LANES), lambda i, *_, e=e: (e, 0)) for e in ends]
        pack_rows += count * HALO
        edges += [part, part]
    slots = (owners, capacity * width + 8, LANES)
    return pl.pallas_call(
        functools.partial(remap_kernel, owners, capacity),
        grid_spec=pltpu.PrefetchScalarGridSpec(
            num_scalar_prefetch=4,
            grid=(block_count // per_step,),
            in_specs=[
                pl.BlockSpec((width, cells), lambda i, *_: (0, 0)),
                pl.BlockSpec((per_step, LANES, LANES), lambda i, *_: (i, 0, 0)),
                *specs,
            ],
            out_specs=[
                pl.BlockSpec(slots, lambda i, *_: (0, 0, 0)),
                pl.BlockSpec((pack_rows, LANES), lambda i, *_: (0, 0)),
                pl.BlockSpec((pack_rows, LANES), lambda i, *_: (0, 0)),
            ],
            scratch_shapes=[
                pltpu.SMEM((owners,), jnp.int32),
                pltpu.VMEM((owners, LANES), F32),
            ],
        ),
        out_shape=[
            jax.ShapeDtypeStruct(slots, F32),
            jax.ShapeDtypeStruct((pack_rows, LANES), F32),
            jax.ShapeDtypeStruct((pack_rows, LANES), F32),
        ],
        compiler_params=pltpu.CompilerParams(vmem_limit_bytes=60 * MIB),
        name="remap",
    )(routes, target, source, me, fields, weights, *edges)


def assemble_kernel(owners, capacity, width, slots, out, low, high, hot, values):
    rows = out.shape[1]
    count = owners * capacity
    per_row = LANES // capacity
    size = capacity * width
    pitch = size + 8
    block = lax.broadcasted_iota(jnp.int32, (rows, LANES), 0) + 1
    for sender in range(owners):
        values[sender * size : (sender + 1) * size, :] = slots[
            sender * pitch : sender * pitch + size, :
        ]
    for half in range(count // LANES):
        label = None
        for sender in range(half * per_row, (half + 1) * per_row):
            row = slots[sender * pitch + size : sender * pitch + size + 1, :]
            label = row if label is None else label + row
        label = jnp.broadcast_to(label.astype(jnp.int32), (rows, LANES))
        hot[:, half * LANES : (half + 1) * LANES] = (label == block).astype(F32).astype(BF16)
    picks = hot[...]
    for field in range(width):
        value_high, value_low = split(values[pl.ds(field, count, stride=width), :])
        both = jnp.concatenate([value_high, value_low], axis=1)
        total = jnp.dot(picks, both, preferred_element_type=F32)
        total = total[:, :LANES] + total[:, LANES:]
        out[field] = total
        low[field] = total[:HALO]
        high[field] = total[rows - HALO :]


def assemble(slots, owners, capacity, width, rows):
    return pl.pallas_call(
        functools.partial(assemble_kernel, owners, capacity, width),
        out_shape=[
            jax.ShapeDtypeStruct((width, rows, LANES), F32),
            jax.ShapeDtypeStruct((width, HALO, LANES), F32),
            jax.ShapeDtypeStruct((width, HALO, LANES), F32),
        ],
        scratch_shapes=[
            pltpu.VMEM((rows, owners * capacity), BF16),
            pltpu.VMEM((owners * capacity * width, LANES), F32),
        ],
        compiler_params=pltpu.CompilerParams(vmem_limit_bytes=12 * MIB),
        name="assemble",
    )(slots)


def lane_pick(value, index):
    return jnp.take_along_axis(value, index, axis=1, mode="promise_in_bounds")


def group_rows(chunk, chunks):
    base = chunk * CHUNK
    late = (chunk > chunks // 2).astype(jnp.int32) * GROUP
    return pl.multiple_of(base + GROUP - late, GROUP), pl.multiple_of(base + late, GROUP)


def to_lanes(levels, column, wide, row):
    pitch = column.shape[0] // levels
    here = pl.ds(pl.multiple_of((row + PAD) * LANES, LANES), LANES)
    tiles = [
        column[pl.ds(level * pitch + PAD + row, 8, stride=pitch), :]
        for level in range(0, levels, 8)
    ]
    high, low = split(jnp.concatenate(tiles, axis=0))
    wide[0:levels, here] = high
    wide[levels : 2 * levels, here] = low


def spread_tile(levels, total, wide, matrix, entry, row, mix):
    at = pl.multiple_of((row + PAD - REACH) * LANES, LANES)
    got = jnp.dot(
        wide[:, pl.ds(at, WINDOW * LANES)],
        jnp.concatenate([part[entry] for part in matrix], axis=0),
        preferred_element_type=F32,
    )
    got = got[:, :LANES] + got[:, LANES:]
    got = got[:levels] + got[levels:]
    for level in range(0, levels, 8):
        mix[pl.ds(level * total + row, 8, stride=total), :] = got[level : level + 8]


def spread_group(levels, total, column, row, terms, mix, out=None, step=None):
    pitch = column.shape[0] // levels
    right = [None] * levels
    for which in range(NB):
        index, code, factor = terms(which)
        for level in range(levels):
            found = None
            for reach in range(WINDOW):
                at = level * pitch + PAD - REACH + reach + row
                picked = lane_pick(column[pl.ds(at, GROUP), :], index)
                found = picked if found is None else jnp.where(code == reach, picked, found)
            found = factor * found
            right[level] = found if which == 0 else right[level] + found
    out, step = (row, total) if out is None else (out, step)
    for level in range(levels):
        mix[pl.ds(level * step + out, GROUP), :] = right[level]


def edge_row(index, total):
    far = (index >= 2).astype(jnp.int32)
    return pl.multiple_of(index * GROUP + far * (total - 4 * GROUP), GROUP)


def spots_of(offset):
    return offset + lax.broadcasted_iota(jnp.int32, offset.shape, offset.ndim - 1) + RIM


def lane_of(spot):
    return jnp.bitwise_and(spot, LANES - 1)


def code_of(spot):
    return lax.shift_right_logical(spot, LANES.bit_length() - 1)


def state_rows(state, column, row):
    levels = state.shape[0]
    pitch = column.shape[0] // levels
    here = pl.ds(pl.multiple_of(row * LANES, LANES), LANES)
    for level in range(0, levels, 8):
        at = level * pitch + PAD + HALO + row
        column[pl.ds(at, 8, stride=pitch), :] = state[level : level + 8, here]


def build_kernel(state, coef, offset, wet, mix, *refs):
    matrix, (column, wide, spots, highs, lows) = refs[:WINDOW], refs[WINDOW:]
    chunk = pl.program_id(0)
    chunks = pl.num_programs(0)
    levels = state.shape[0]
    rows = state.shape[1] // LANES
    total = rows + 2 * HALO

    @pl.when(chunk == 0)
    def _():
        @pl.loop(0, rows, unroll=8)
        def _(row):
            state_rows(state, column, row)

        @pl.loop(0, rows, unroll=8)
        def _(row):
            to_lanes(levels, column, wide, row + HALO)

        mix[pl.ds(levels * total + HALO, rows), :] = wet[...].astype(F32) * force_scale

    by_matrix, by_gather = group_rows(chunk, chunks)
    here = pl.ds(pl.multiple_of(by_matrix - HALO, GROUP), GROUP)
    spot = [spots_of(offset[which, here, :]) for which in range(NB)]
    factor = [coef[which, here, :] for which in range(NB)]
    for which in range(NB):
        spots[which] = spot[which]
        joint = factor[which]
        for other in range(NB):
            if other != which:
                joint = joint + jnp.where(spot[other] == spot[which], factor[other], 0.0)
        high = joint.astype(BF16).astype(F32)
        highs[which] = high
        lows[which] = joint - high

    inside = (chunk > 0) & (chunk < chunks - 1)
    near = pl.ds(pl.multiple_of(jnp.where(inside, by_gather - HALO, 0), GROUP), GROUP)

    def terms(which):
        spot = spots_of(offset[which, near, :])
        return lane_of(spot), code_of(spot), coef[which, near, :]

    spread_group(levels, total, column, by_gather, terms, mix)

    small = jnp.int16

    @pl.loop(0, GROUP, unroll=8)
    def _(tile):
        def wide_row(ref, kind):
            return [
                jnp.broadcast_to(ref[which, pl.ds(tile, 1), :], (16, LANES)).astype(kind)
                for which in range(NB)
            ]

        spot_rows, high_rows, low_rows = (
            wide_row(spots, small),
            wide_row(highs, BF16),
            wide_row(lows, BF16),
        )
        count = lax.broadcasted_iota(jnp.int32, (16, LANES), 0).astype(small)
        for first in range(0, WINDOW * LANES, 16):
            key = count + small(first)
            by_high = jnp.zeros((16, LANES), BF16)
            by_low = jnp.zeros((16, LANES), BF16)
            for which in range(NB):
                hit = spot_rows[which] == key
                by_high = jnp.where(hit, high_rows[which], by_high)
                by_low = jnp.where(hit, low_rows[which], by_low)
            part, at = matrix[first // LANES], first % LANES
            part[tile, at : at + 16, 0:LANES] = by_high
            part[tile, at : at + 16, LANES : 2 * LANES] = by_low

    for tile in range(GROUP):
        spread_tile(levels, total, wide, matrix, tile, by_matrix + tile, mix)


def build(state, coef, offset, wet):
    levels, cells = state.shape
    rows = cells // LANES
    total = rows + 2 * HALO
    pitch = total + 2 * PAD
    chunks = total // CHUNK
    span = WINDOW * LANES
    return pl.pallas_call(
        build_kernel,
        grid=(chunks,),
        in_specs=[
            pl.BlockSpec(state.shape, lambda i: (0, 0)),
            pl.BlockSpec(coef.shape, lambda i: (0, 0, 0)),
            pl.BlockSpec(offset.shape, lambda i: (0, 0, 0)),
            pl.BlockSpec(wet.shape, lambda i: (0, 0)),
        ],
        out_specs=[
            pl.BlockSpec(((levels + 1) * total, LANES), lambda i: (0, 0)),
            *[pl.BlockSpec((GROUP, LANES, 2 * LANES), lambda i: (i, 0, 0))] * WINDOW,
        ],
        out_shape=[
            jax.ShapeDtypeStruct(((levels + 1) * total, LANES), F32),
            *[jax.ShapeDtypeStruct((chunks * GROUP, LANES, 2 * LANES), BF16)] * WINDOW,
        ],
        scratch_shapes=[
            pltpu.VMEM((levels * pitch, LANES), F32),
            pltpu.VMEM((2 * levels, pitch * LANES), BF16),
            pltpu.VMEM((NB, GROUP, LANES), jnp.int32),
            pltpu.VMEM((NB, GROUP, LANES), F32),
            pltpu.VMEM((NB, GROUP, LANES), F32),
        ],
        compiler_params=pltpu.CompilerParams(vmem_limit_bytes=56 * MIB),
        cost_estimate=pl.CostEstimate(
            flops=2 * chunks * GROUP * 2 * levels * span * 2 * LANES,
            bytes_accessed=80 * MIB,
            transcendentals=0,
        ),
        name="build",
    )(state, coef, offset, wet)


def prepare_kernel(
    state, coef, offset, vert, low_far, high_far, *refs
):
    far, (column, edge, inv, from_up, from_down, lanes, codes, coefs, keep, *refs) = (
        refs[:WINDOW],
        refs[WINDOW:],
    )
    matrix, (verts, low, high, packed, copied) = refs[:WINDOW], refs[WINDOW:]
    pack_copies = [
        pltpu.make_async_copy(source, target, packed.at[index])
        for index, (source, target) in enumerate(((low_far, low), (high_far, high)))
    ]
    matrix_copies = [
        pltpu.make_async_copy(far[reach], matrix[reach], copied.at[reach])
        for reach in range(WINDOW)
    ]
    for copy in pack_copies + matrix_copies:
        copy.start()
    levels = state.shape[0]
    rows = state.shape[1] // LANES
    total = rows + 2 * HALO
    pitch = column.shape[0] // levels
    inner = levels - 1
    pieces = levels * GROUP

    main = slice(HALO, HALO + rows)
    coefs[:, main, :] = coef[...]
    lanes[:, main, :] = offset[...]
    verts[:, main, :] = vert[...]

    @pl.loop(0, rows, unroll=8)
    def _(row):
        state_rows(state, column, row)

    for copy in pack_copies:
        copy.wait()
    for pack, first in ((low, 0), (high, total - HALO)):
        for level in range(levels):
            at = level * pitch + PAD + first
            column[at : at + HALO, :] = pack[level * HALO : (level + 1) * HALO, :]
        here = slice(first, first + HALO)
        at = levels * HALO
        for out, count in ((coefs, NB), (lanes, NB), (verts, inner)):
            for index in range(count):
                out[index, here, :] = pack[at : at + HALO, :].astype(out.dtype)
                at += HALO
        to = 4 * pieces + (0 if first == 0 else HALO)
        edge[to : to + HALO, :] = pack[at : at + HALO, :] * force_scale

    @pl.loop(0, total // GROUP)
    def _(group):
        here = pl.ds(pl.multiple_of(group * GROUP, GROUP), GROUP)
        left = 1.0
        for which in range(NB):
            spot = spots_of(lanes[which, here, :])
            lanes[which, here, :] = lane_of(spot)
            codes[which, here, :] = code_of(spot)
            left = left - coefs[which, here, :]
        keep[here, :] = left
        upper = jnp.zeros((GROUP, LANES), F32)
        carried = jnp.zeros((GROUP, LANES), F32)
        for level in range(levels):
            lower = verts[level, here, :] if level < inner else jnp.zeros((GROUP, LANES), F32)
            pivot = (1.0 + upper + lower) - upper * carried
            inverse = 1.0 / pivot
            carried = lower * inverse
            inv[level, here, :] = inverse
            from_up[level, here, :] = upper * inverse
            from_down[level, here, :] = carried
            upper = lower

    @pl.loop(0, 4)
    def _(index):
        row = edge_row(index, total)
        here = pl.ds(row, GROUP)

        def terms(which):
            return lanes[which, here, :], codes[which, here, :], coefs[which, here, :]

        spread_group(levels, total, column, row, terms, edge, index * pieces, GROUP)

    for copy in matrix_copies:
        copy.wait()


def prepare(state, coef, offset, vert, low, high, matrix):
    levels, cells = state.shape
    rows = cells // LANES
    total = rows + 2 * HALO
    pitch = total + 2 * PAD
    level_shape = pltpu.VMEM((levels, total, LANES), F32)
    index_shape = pltpu.VMEM((NB, total, LANES), jnp.int32)
    near = pl.BlockSpec(memory_space=pltpu.VMEM)
    far = pl.BlockSpec(memory_space=pltpu.HBM)
    low, high, *matrix = [
        pltpu.with_memory_space_constraint(part, pltpu.HBM) for part in (low, high, *matrix)
    ]
    return pl.pallas_call(
        prepare_kernel,
        out_shape=[
            pltpu.VMEM((levels * pitch, LANES), F32),
            pltpu.VMEM((4 * levels * GROUP + 2 * HALO, LANES), F32),
            level_shape,
            level_shape,
            level_shape,
            index_shape,
            index_shape,
            pltpu.VMEM((NB, total, LANES), F32),
            pltpu.VMEM((total, LANES), F32),
            *[pltpu.VMEM(part.shape, part.dtype) for part in matrix],
        ],
        in_specs=[near] * 4 + [far] * (2 + WINDOW),
        out_specs=[near] * (9 + WINDOW),
        scratch_shapes=[
            pltpu.VMEM((levels - 1, total, LANES), F32),
            pltpu.VMEM(low.shape, F32),
            pltpu.VMEM(high.shape, F32),
            pltpu.SemaphoreType.DMA((2,)),
            pltpu.SemaphoreType.DMA((WINDOW,)),
        ],
        compiler_params=pltpu.CompilerParams(vmem_limit_bytes=12 * MIB),
        cost_estimate=pl.CostEstimate(flops=0, bytes_accessed=16 * MIB, transcendentals=0),
        name="prepare",
    )(state, coef, offset, vert, low, high, *matrix)


def interval_kernel(
    width, early, column, edge, inv, from_up, from_down, lanes, codes, coefs, keep, *refs
):
    matrix, refs = refs[:WINDOW], refs[WINDOW:]
    imported, low, high, state_out, imported_out, *refs = refs
    cells, mixed, wide, force, flat, wets = refs
    levels, total = inv.shape[0], inv.shape[1]
    rows = total - 2 * HALO
    pitch = column.shape[0] // levels
    chunks = total // CHUNK

    pieces = levels * GROUP
    mixed[...] = early[0 : levels * total, :]
    wets[...] = early[levels * total : (levels + 1) * total, :]
    wets[0:HALO, :] = edge[4 * pieces : 4 * pieces + HALO, :]
    wets[HALO + rows : total, :] = edge[4 * pieces + HALO : 4 * pieces + 2 * HALO, :]
    for index in range(4):
        row = index * GROUP + (total - 4 * GROUP if index >= 2 else 0)
        for level in range(levels):
            to, at = level * total + row, index * pieces + level * GROUP
            mixed[to : to + GROUP, :] = edge[at : at + GROUP, :]

    force[:, 0:HALO, :] = low[...]
    force[:, HALO : HALO + rows, :] = imported[...]
    force[:, HALO + rows : total, :] = high[...]
    for field in range(width):
        flat[pl.ds(field * rows, rows), :] = imported[field]

    @pl.loop(0, rows, unroll=8)
    def _(row):
        here = pl.ds(pl.multiple_of(row * LANES, LANES), LANES)
        imported_out[:, here] = flat[pl.ds(row, width, stride=rows), :]

    def solve(chunk, source, spread_sum, out, wide):
        for group in range(CHUNK // GROUP):
            row = pl.multiple_of(chunk * CHUNK + group * GROUP, GROUP)
            here = pl.ds(row, GROUP)
            left = keep[here, :]
            wet = wets[here, :]
            partial = []
            for level in range(levels):
                value = left * source[pl.ds(level * pitch + PAD + row, GROUP), :]
                value = value + spread_sum[pl.ds(level * total + row, GROUP), :]
                if level < width:
                    value = value + force[level, here, :] * wet
                value = value * inv[level, here, :]
                if level:
                    value = value + from_up[level, here, :] * partial[-1]
                partial.append(value)
            following = partial[-1]
            out[pl.ds((levels - 1) * pitch + PAD + row, GROUP), :] = following
            for level in range(levels - 2, -1, -1):
                following = partial[level] + from_down[level, here, :] * following
                out[pl.ds(level * pitch + PAD + row, GROUP), :] = following
        for row in range(CHUNK):
            to_lanes(levels, out, wide, chunk * CHUNK + row)

    def spread(chunk, source, wide):
        by_matrix, by_gather = group_rows(chunk, chunks)
        for tile in range(GROUP):
            spread_tile(
                levels, total, wide, matrix, chunk * GROUP + tile, by_matrix + tile, mixed
            )
        here = pl.ds(by_gather, GROUP)

        def terms(which):
            return lanes[which, here, :], codes[which, here, :], coefs[which, here, :]

        spread_group(levels, total, source, by_gather, terms, mixed)

    @pl.loop(0, chunks)
    def _(chunk):
        solve(chunk, column, mixed, cells, wide)

    @pl.loop(1, STEPS)
    def _(step):
        for chunk in range(chunks):
            spread(jnp.int32(chunk), cells, wide)
        for chunk in range(chunks):
            solve(chunk, cells, mixed, cells, wide)

    @pl.loop(0, rows, unroll=8)
    def _(row):
        here = pl.ds(pl.multiple_of(row * LANES, LANES), LANES)
        for level in range(0, levels, 8):
            at = level * pitch + PAD + HALO + row
            state_out[level : level + 8, here] = cells[pl.ds(at, 8, stride=pitch), :]


def interval(early, column, edge, inv, *rest):
    levels, total = inv.shape[0], inv.shape[1]
    pitch = column.shape[0] // levels
    width, rows = rest[-3].shape[0], rest[-3].shape[1]
    operands = (early, column, edge, inv, *rest)
    return pl.pallas_call(
        functools.partial(interval_kernel, width),
        out_shape=[
            jax.ShapeDtypeStruct((levels, rows * LANES), F32),
            jax.ShapeDtypeStruct((width, rows * LANES), F32),
        ],
        in_specs=[pl.BlockSpec(memory_space=pltpu.VMEM)] * len(operands),
        out_specs=[pl.BlockSpec(memory_space=pltpu.VMEM)] * 2,
        scratch_shapes=[
            pltpu.VMEM(column.shape, F32),
            pltpu.VMEM((levels * total, LANES), F32),
            pltpu.VMEM((2 * levels, pitch * LANES), BF16),
            pltpu.VMEM((width, total, LANES), F32),
            pltpu.VMEM((width * rows, LANES), F32),
            pltpu.VMEM((total, LANES), F32),
        ],
        compiler_params=pltpu.CompilerParams(vmem_limit_bytes=12 * MIB),
        name="interval",
    )(*operands)


def local(
    state,
    export_fields,
    remap_weights,
    routes,
    target_block,
    source_block,
    wet_mask,
    edge_coeff,
    edge_offset,
    vert_coeff,
):
    owners = lax.axis_size("dom")
    comps = lax.axis_size("comp")
    cells = state.shape[2]
    block_count = remap_weights.shape[1]
    capacity = max(2, 2 * block_count // owners)
    width = export_fields.shape[1]
    rows = cells // LANES
    me = lax.axis_index("dom").astype(jnp.int32)[None]
    coef = edge_coeff[0].reshape(-1, rows, LANES)
    offset = edge_offset[0].reshape(-1, rows, LANES)
    vert = vert_coeff[0].reshape(-1, rows, LANES)
    wet = wet_mask.reshape(rows, LANES)

    values, low, high = remap(
        routes[0, :, 0],
        target_block[0],
        source_block[0],
        me,
        export_fields[0],
        remap_weights[0],
        state[0],
        (coef, offset, vert, wet),
        owners,
        capacity,
    )
    values = lax.all_to_all(values, "dom", split_axis=0, concat_axis=0, tiled=True)

    forward = [(i, (i + 1) % owners) for i in range(owners)]
    backward = [(target, source) for source, target in forward]
    low = lax.ppermute(low, "dom", forward)
    high = lax.ppermute(high, "dom", backward)
    built = build(state[0], coef, offset, wet)
    values, built, low, high = lax.optimization_barrier((values, built, low, high))
    early, *matrix = built
    early = pltpu.with_memory_space_constraint(early, pltpu.VMEM)

    pitch = capacity * width + 8
    summed, first_rows, last_rows = assemble(
        values.reshape(owners * pitch, LANES), owners, capacity, width, rows
    )

    def across(value, shift):
        pairs = [
            (comp * owners + dom, (comp + 1) % comps * owners + (dom + shift) % owners)
            for comp in range(comps)
            for dom in range(owners)
        ]
        return lax.ppermute(value, ("comp", "dom"), pairs)

    imported = across(summed, 0)
    from_low = across(last_rows, 1)
    from_high = across(first_rows, -1)
    prepared = prepare(state[0], coef, offset, vert, low, high, matrix)
    new_state, imported = interval(early, *prepared, imported, from_low, from_high)
    return (new_state[None], imported[None])


def solution(mesh):
    placed = (
        P("comp", None, "dom"),
        P("comp", None, "dom"),
        P("comp", "dom", None, None),
        P("comp", "dom", None),
        P("comp", "dom"),
        P("comp", "dom"),
        P("comp", "dom"),
        P("comp", None, "dom"),
        P("comp", None, "dom"),
        P("comp", None, "dom"),
    )
    return jax.shard_map(
        local,
        mesh=mesh,
        in_specs=placed,
        out_specs=(P("comp", None, "dom"), P("comp", None, "dom")),
        check_vma=False,
    )
```

```python
import functools

import jax
import jax.numpy as jnp
from jax import lax
from jax.experimental import pallas as pl
from jax.experimental.pallas import tpu as pltpu
from jax.sharding import PartitionSpec as P

NB = 6
RIM = 256
STEPS = 4
LANES = 128
REACH = RIM // LANES
WINDOW = 2 * REACH + 1
EARLY = WINDOW - REACH
HALO = STEPS * REACH
PAD = 8
MIB = 2**20
GROUP = 8
CHUNK = 2 * GROUP

force_scale = 0.5

F32 = jnp.float32
BF16 = jnp.bfloat16


def split(value):
    high = value.astype(BF16)
    return high, (value - high.astype(F32)).astype(BF16)


def remap_kernel(
    owners, capacity, routes, target, source, me, fields_far, weights_far, *refs
):
    far, (out, low, high, fields, weights, *refs) = refs[:5], refs[5:]
    near, (counts, marks, filled, loaded) = refs[:10], refs[10:]
    block_count = weights.shape[0]
    per_step = 16
    width = fields.shape[0]
    levels, cells = far[0].shape
    rows = cells // LANES
    edge = HALO * LANES
    lane = lax.broadcasted_iota(jnp.int32, (1, LANES), 1)
    label_row = capacity * width

    def chunk_copy(step):
        here = pl.ds(step * per_step, per_step)
        return pltpu.make_async_copy(weights_far.at[here], weights.at[here], loaded.at[step])

    fields_copy = pltpu.make_async_copy(fields_far, fields, filled.at[10])
    fields_copy.start()
    for step in range(block_count // per_step):
        chunk_copy(step).start()
    edge_copies = []
    for index, part in enumerate(far):
        for side in range(2):
            if index == 0:
                piece = part.at[:, pl.ds((0 if side else cells - edge), edge)]
            elif len(part.shape) == 3:
                piece = part.at[:, pl.ds((0 if side else rows - HALO), HALO), :]
            else:
                piece = part.at[pl.ds((0 if side else rows - HALO), HALO), :]
            at = 2 * index + side
            edge_copies.append(pltpu.make_async_copy(piece, near[at], filled.at[at]))
            edge_copies[-1].start()

    out[...] = jnp.zeros_like(out)
    marks[...] = jnp.zeros_like(marks)
    for owner in range(owners):
        counts[owner] = 0
    fields_copy.wait()

    @pl.loop(0, block_count // per_step)
    def _(step):
        chunk_copy(step).wait()
        remap_blocks(
            capacity, step * per_step, per_step, routes, target, source, me, fields, weights,
            out, counts, marks, lane,
        )

    for owner in range(owners):
        out[owner, label_row : label_row + 1, :] = marks[owner : owner + 1, :]
    for copy in edge_copies:
        copy.wait()
    for side, pack in ((0, low), (1, high)):
        state, coef, offset, vert, wet = near[side::2]
        for row in range(HALO):
            for level in range(0, levels, 8):
                tile = state[level : level + 8, row * LANES : (row + 1) * LANES]
                pack[pl.ds(level * HALO + row, 8, stride=HALO), :] = tile
        at = levels * HALO
        for part in (coef, offset, vert):
            for index in range(part.shape[0]):
                pack[at : at + HALO, :] = part[index].astype(F32)
                at += HALO
        pack[at : at + HALO, :] = wet[...].astype(F32)


def remap_blocks(
    capacity, first, count, routes, target, source, me, fields, weights, out, counts, marks, lane
):
    width = fields.shape[0]
    for index in range(count):
        block = first + index
        owner = routes[block]
        rank = counts[owner]
        counts[owner] = rank + 1
        start = pl.multiple_of(source[block] * LANES, LANES)
        picked_high, picked_low = split(fields[:, pl.ds(start, LANES)])
        picked = jnp.concatenate([picked_high, picked_low], axis=0)
        both = jnp.concatenate(split(weights[block]), axis=1)
        product = jnp.dot(picked, both, preferred_element_type=F32)
        product = product[:, :LANES] + product[:, LANES:]
        value = product[:width] + product[width:]
        row = pl.multiple_of(rank * width, width)
        out[owner, pl.ds(row, width), :] = value
        slot = lax.rem(me[0] * capacity + rank, LANES)
        marks[pl.ds(owner, 1), :] = jnp.where(
            lane == slot, (target[block] + 1).astype(F32), marks[pl.ds(owner, 1), :]
        )


def remap(routes, target, source, me, fields, weights, state, parts, owners, capacity):
    block_count = weights.shape[0]
    width = fields.shape[0]
    levels = state.shape[0]
    scratch = [pltpu.VMEM((levels, HALO * LANES), F32)] * 2
    pack_rows = levels * HALO
    for part in parts:
        count = part.shape[0] if part.ndim == 3 else 1
        scratch += [pltpu.VMEM((*part.shape[:-2], HALO, LANES), part.dtype)] * 2
        pack_rows += count * HALO
    slots = (owners, capacity * width + 8, LANES)
    scalar = pl.BlockSpec(memory_space=pltpu.SMEM)
    far = pl.BlockSpec(memory_space=pltpu.HBM)
    near = pl.BlockSpec(memory_space=pltpu.VMEM)
    return pl.pallas_call(
        functools.partial(remap_kernel, owners, capacity),
        in_specs=[scalar] * 4 + [far] * 7,
        out_specs=[near] * 3,
        out_shape=[
            jax.ShapeDtypeStruct(slots, F32),
            jax.ShapeDtypeStruct((pack_rows, LANES), F32),
            jax.ShapeDtypeStruct((pack_rows, LANES), F32),
        ],
        scratch_shapes=[
            pltpu.VMEM(fields.shape, F32),
            pltpu.VMEM(weights.shape, F32),
            *scratch,
            pltpu.SMEM((owners,), jnp.int32),
            pltpu.VMEM((owners, LANES), F32),
            pltpu.SemaphoreType.DMA((11,)),
            pltpu.SemaphoreType.DMA((block_count // 16,)),
        ],
        compiler_params=pltpu.CompilerParams(vmem_limit_bytes=60 * MIB),
        name="remap",
    )(routes, target, source, me, fields, weights, state, *parts)


def assemble_kernel(owners, capacity, width, slots, out, low, high, hot, values):
    rows = out.shape[1]
    count = owners * capacity
    per_row = LANES // capacity
    size = capacity * width
    pitch = size + 8
    block = lax.broadcasted_iota(jnp.int32, (rows, LANES), 0) + 1
    for sender in range(owners):
        values[sender * size : (sender + 1) * size, :] = slots[
            sender * pitch : sender * pitch + size, :
        ]
    for half in range(count // LANES):
        label = None
        for sender in range(half * per_row, (half + 1) * per_row):
            row = slots[sender * pitch + size : sender * pitch + size + 1, :]
            label = row if label is None else label + row
        label = jnp.broadcast_to(label.astype(jnp.int32), (rows, LANES))
        hot[:, half * LANES : (half + 1) * LANES] = (label == block).astype(F32).astype(BF16)
    picks = hot[...]
    for field in range(width):
        value_high, value_low = split(values[pl.ds(field, count, stride=width), :])
        both = jnp.concatenate([value_high, value_low], axis=1)
        total = jnp.dot(picks, both, preferred_element_type=F32)
        total = total[:, :LANES] + total[:, LANES:]
        out[field] = total
        low[field] = total[:HALO]
        high[field] = total[rows - HALO :]


def assemble(slots, owners, capacity, width, rows):
    return pl.pallas_call(
        functools.partial(assemble_kernel, owners, capacity, width),
        out_shape=[
            jax.ShapeDtypeStruct((width, rows, LANES), F32),
            jax.ShapeDtypeStruct((width, HALO, LANES), F32),
            jax.ShapeDtypeStruct((width, HALO, LANES), F32),
        ],
        scratch_shapes=[
            pltpu.VMEM((rows, owners * capacity), BF16),
            pltpu.VMEM((owners * capacity * width, LANES), F32),
        ],
        compiler_params=pltpu.CompilerParams(vmem_limit_bytes=12 * MIB),
        name="assemble",
    )(slots)


def lane_pick(value, index):
    return jnp.take_along_axis(value, index, axis=1, mode="promise_in_bounds")


def group_rows(chunk, chunks):
    base = chunk * CHUNK
    late = (chunk > chunks // 2).astype(jnp.int32) * GROUP
    return pl.multiple_of(base + GROUP - late, GROUP), pl.multiple_of(base + late, GROUP)


def to_lanes(levels, column, wide, row):
    pitch = column.shape[0] // levels
    here = pl.ds(pl.multiple_of((row + PAD) * LANES, LANES), LANES)
    tiles = [
        column[pl.ds(level * pitch + PAD + row, 8, stride=pitch), :]
        for level in range(0, levels, 8)
    ]
    high, low = split(jnp.concatenate(tiles, axis=0))
    wide[0:levels, here] = high
    wide[levels : 2 * levels, here] = low


def spread_tile(levels, total, wide, matrix, entry, row, mix):
    at = pl.multiple_of((row + PAD - REACH) * LANES, LANES)
    got = jnp.dot(
        wide[:, pl.ds(at, WINDOW * LANES)],
        jnp.concatenate([part[entry] for part in matrix], axis=0),
        preferred_element_type=F32,
    )
    got = got[:, :LANES] + got[:, LANES:]
    got = got[:levels] + got[levels:]
    for level in range(0, levels, 8):
        mix[pl.ds(level * total + row, 8, stride=total), :] = got[level : level + 8]


def spread_group(levels, total, column, row, terms, mix, out=None, step=None):
    pitch = column.shape[0] // levels
    right = [None] * levels
    for which in range(NB):
        index, code, factor = terms(which)
        for level in range(levels):
            found = None
            for reach in range(WINDOW):
                at = level * pitch + PAD - REACH + reach + row
                picked = lane_pick(column[pl.ds(at, GROUP), :], index)
                found = picked if found is None else jnp.where(code == reach, picked, found)
            found = factor * found
            right[level] = found if which == 0 else right[level] + found
    out, step = (row, total) if out is None else (out, step)
    for level in range(levels):
        mix[pl.ds(level * step + out, GROUP), :] = right[level]


def edge_row(index, total):
    far = (index >= 2).astype(jnp.int32)
    return pl.multiple_of(index * GROUP + far * (total - 4 * GROUP), GROUP)


def spots_of(offset):
    return offset + lax.broadcasted_iota(jnp.int32, offset.shape, offset.ndim - 1) + RIM


def lane_of(spot):
    return jnp.bitwise_and(spot, LANES - 1)


def code_of(spot):
    return lax.shift_right_logical(spot, LANES.bit_length() - 1)


def state_rows(state, column, row):
    levels = state.shape[0]
    pitch = column.shape[0] // levels
    here = pl.ds(pl.multiple_of(row * LANES, LANES), LANES)
    for level in range(0, levels, 8):
        at = level * pitch + PAD + HALO + row
        column[pl.ds(at, 8, stride=pitch), :] = state[level : level + 8, here]


def build_kernel(state, coef, offset, wet, mix, *refs):
    matrix, (column, wide, spots, highs, lows) = refs[:WINDOW], refs[WINDOW:]
    chunk = pl.program_id(0)
    chunks = pl.num_programs(0)
    levels = state.shape[0]
    rows = state.shape[1] // LANES
    total = rows + 2 * HALO

    @pl.when(chunk == 0)
    def _():
        @pl.loop(0, rows, unroll=8)
        def _(row):
            state_rows(state, column, row)

        @pl.loop(0, rows, unroll=8)
        def _(row):
            to_lanes(levels, column, wide, row + HALO)

        mix[pl.ds(levels * total + HALO, rows), :] = wet[...].astype(F32) * force_scale

    by_matrix, by_gather = group_rows(chunk, chunks)
    here = pl.ds(pl.multiple_of(by_matrix - HALO, GROUP), GROUP)
    spot = [spots_of(offset[which, here, :]) for which in range(NB)]
    factor = [coef[which, here, :] for which in range(NB)]
    for which in range(NB):
        spots[which] = spot[which]
        joint = factor[which]
        for other in range(NB):
            if other != which:
                joint = joint + jnp.where(spot[other] == spot[which], factor[other], 0.0)
        high = joint.astype(BF16).astype(F32)
        highs[which] = high
        lows[which] = joint - high

    inside = (chunk > 0) & (chunk < chunks - 1)
    near = pl.ds(pl.multiple_of(jnp.where(inside, by_gather - HALO, 0), GROUP), GROUP)

    def terms(which):
        spot = spots_of(offset[which, near, :])
        return lane_of(spot), code_of(spot), coef[which, near, :]

    spread_group(levels, total, column, by_gather, terms, mix)

    small = jnp.int16

    @pl.loop(0, GROUP, unroll=8)
    def _(tile):
        def wide_row(ref, kind):
            return [
                jnp.broadcast_to(ref[which, pl.ds(tile, 1), :], (16, LANES)).astype(kind)
                for which in range(NB)
            ]

        spot_rows, high_rows, low_rows = (
            wide_row(spots, small),
            wide_row(highs, BF16),
            wide_row(lows, BF16),
        )
        count = lax.broadcasted_iota(jnp.int32, (16, LANES), 0).astype(small)
        for first in range(0, WINDOW * LANES, 16):
            key = count + small(first)
            by_high = jnp.zeros((16, LANES), BF16)
            by_low = jnp.zeros((16, LANES), BF16)
            for which in range(NB):
                hit = spot_rows[which] == key
                by_high = jnp.where(hit, high_rows[which], by_high)
                by_low = jnp.where(hit, low_rows[which], by_low)
            part, at = matrix[first // LANES], first % LANES
            part[tile, at : at + 16, 0:LANES] = by_high
            part[tile, at : at + 16, LANES : 2 * LANES] = by_low

    for tile in range(GROUP):
        spread_tile(levels, total, wide, matrix, tile, by_matrix + tile, mix)


def build(state, coef, offset, wet):
    levels, cells = state.shape
    rows = cells // LANES
    total = rows + 2 * HALO
    pitch = total + 2 * PAD
    chunks = total // CHUNK
    span = WINDOW * LANES
    return pl.pallas_call(
        build_kernel,
        grid=(chunks,),
        in_specs=[
            pl.BlockSpec(state.shape, lambda i: (0, 0)),
            pl.BlockSpec(coef.shape, lambda i: (0, 0, 0)),
            pl.BlockSpec(offset.shape, lambda i: (0, 0, 0)),
            pl.BlockSpec(wet.shape, lambda i: (0, 0)),
        ],
        out_specs=[
            pl.BlockSpec(((levels + 1) * total, LANES), lambda i: (0, 0)),
            *[pl.BlockSpec((GROUP, LANES, 2 * LANES), lambda i: (i, 0, 0))] * WINDOW,
        ],
        out_shape=[
            jax.ShapeDtypeStruct(((levels + 1) * total, LANES), F32),
            *[jax.ShapeDtypeStruct((chunks * GROUP, LANES, 2 * LANES), BF16)] * WINDOW,
        ],
        scratch_shapes=[
            pltpu.VMEM((levels * pitch, LANES), F32),
            pltpu.VMEM((2 * levels, pitch * LANES), BF16),
            pltpu.VMEM((NB, GROUP, LANES), jnp.int32),
            pltpu.VMEM((NB, GROUP, LANES), F32),
            pltpu.VMEM((NB, GROUP, LANES), F32),
        ],
        compiler_params=pltpu.CompilerParams(vmem_limit_bytes=56 * MIB),
        cost_estimate=pl.CostEstimate(
            flops=2 * chunks * GROUP * 2 * levels * span * 2 * LANES,
            bytes_accessed=80 * MIB,
            transcendentals=0,
        ),
        name="build",
    )(state, coef, offset, wet)


def prepare_kernel(
    state, coef, offset, vert, low_far, high_far, *refs
):
    far, (column, edge, inv, from_up, from_down, lanes, codes, coefs, keep, *refs) = (
        refs[:EARLY],
        refs[EARLY:],
    )
    matrix, (verts, low, high, packed, copied) = refs[:EARLY], refs[EARLY:]
    pack_copies = [
        pltpu.make_async_copy(source, target, packed.at[index])
        for index, (source, target) in enumerate(((low_far, low), (high_far, high)))
    ]
    matrix_copies = [
        pltpu.make_async_copy(far[reach], matrix[reach], copied.at[reach])
        for reach in range(EARLY)
    ]
    for copy in pack_copies:
        copy.start()
    levels = state.shape[0]
    rows = state.shape[1] // LANES
    total = rows + 2 * HALO
    pitch = column.shape[0] // levels
    inner = levels - 1
    pieces = levels * GROUP

    main = slice(HALO, HALO + rows)
    coefs[:, main, :] = coef[...]
    lanes[:, main, :] = offset[...]
    verts[:, main, :] = vert[...]

    @pl.loop(0, rows, unroll=8)
    def _(row):
        state_rows(state, column, row)

    for copy in pack_copies:
        copy.wait()
    for copy in matrix_copies:
        copy.start()
    for pack, first in ((low, 0), (high, total - HALO)):
        for level in range(levels):
            at = level * pitch + PAD + first
            column[at : at + HALO, :] = pack[level * HALO : (level + 1) * HALO, :]
        here = slice(first, first + HALO)
        at = levels * HALO
        for out, count in ((coefs, NB), (lanes, NB), (verts, inner)):
            for index in range(count):
                out[index, here, :] = pack[at : at + HALO, :].astype(out.dtype)
                at += HALO
        to = 4 * pieces + (0 if first == 0 else HALO)
        edge[to : to + HALO, :] = pack[at : at + HALO, :] * force_scale

    @pl.loop(0, total // GROUP)
    def _(group):
        here = pl.ds(pl.multiple_of(group * GROUP, GROUP), GROUP)
        left = 1.0
        for which in range(NB):
            spot = spots_of(lanes[which, here, :])
            lanes[which, here, :] = lane_of(spot)
            codes[which, here, :] = code_of(spot)
            left = left - coefs[which, here, :]
        keep[here, :] = left
        upper = jnp.zeros((GROUP, LANES), F32)
        carried = jnp.zeros((GROUP, LANES), F32)
        for level in range(levels):
            lower = verts[level, here, :] if level < inner else jnp.zeros((GROUP, LANES), F32)
            pivot = (1.0 + upper + lower) - upper * carried
            inverse = 1.0 / pivot
            carried = lower * inverse
            inv[level, here, :] = inverse
            from_up[level, here, :] = upper * inverse
            from_down[level, here, :] = carried
            upper = lower

    @pl.loop(0, 4)
    def _(index):
        row = edge_row(index, total)
        here = pl.ds(row, GROUP)

        def terms(which):
            return lanes[which, here, :], codes[which, here, :], coefs[which, here, :]

        spread_group(levels, total, column, row, terms, edge, index * pieces, GROUP)

    for copy in matrix_copies:
        copy.wait()


def prepare(state, coef, offset, vert, low, high, matrix):
    levels, cells = state.shape
    rows = cells // LANES
    total = rows + 2 * HALO
    pitch = total + 2 * PAD
    level_shape = pltpu.VMEM((levels, total, LANES), F32)
    index_shape = pltpu.VMEM((NB, total, LANES), jnp.int32)
    near = pl.BlockSpec(memory_space=pltpu.VMEM)
    far = pl.BlockSpec(memory_space=pltpu.HBM)
    low, high, *matrix = [
        pltpu.with_memory_space_constraint(part, pltpu.HBM) for part in (low, high, *matrix)
    ]
    return pl.pallas_call(
        prepare_kernel,
        out_shape=[
            pltpu.VMEM((levels * pitch, LANES), F32),
            pltpu.VMEM((4 * levels * GROUP + 2 * HALO, LANES), F32),
            level_shape,
            level_shape,
            level_shape,
            index_shape,
            index_shape,
            pltpu.VMEM((NB, total, LANES), F32),
            pltpu.VMEM((total, LANES), F32),
            *[pltpu.VMEM(part.shape, part.dtype) for part in matrix],
        ],
        in_specs=[near] * 4 + [far] * (2 + EARLY),
        out_specs=[near] * (9 + EARLY),
        scratch_shapes=[
            pltpu.VMEM((levels - 1, total, LANES), F32),
            pltpu.VMEM(low.shape, F32),
            pltpu.VMEM(high.shape, F32),
            pltpu.SemaphoreType.DMA((2,)),
            pltpu.SemaphoreType.DMA((EARLY,)),
        ],
        compiler_params=pltpu.CompilerParams(vmem_limit_bytes=24 * MIB),
        cost_estimate=pl.CostEstimate(flops=0, bytes_accessed=16 * MIB, transcendentals=0),
        name="prepare",
    )(state, coef, offset, vert, low, high, *matrix)


def interval_kernel(
    width, early, column, edge, inv, from_up, from_down, lanes, codes, coefs, keep, *refs
):
    matrix, refs = refs[:EARLY], refs[EARLY:]
    imported, low, high, refs = *refs[:3], refs[3:]
    late_far, (state_out, imported_out, *refs) = refs[: WINDOW - EARLY], refs[WINDOW - EARLY :]
    cells, mixed, wide, force, flat, wets, copied, *late = refs
    matrix = (*matrix, *late)
    late_copies = [
        pltpu.make_async_copy(source, part, copied.at[index])
        for index, (source, part) in enumerate(zip(late_far, late))
    ]
    for copy in late_copies:
        copy.start()
    levels, total = inv.shape[0], inv.shape[1]
    rows = total - 2 * HALO
    pitch = column.shape[0] // levels
    chunks = total // CHUNK

    pieces = levels * GROUP
    wets[...] = early[levels * total : (levels + 1) * total, :]
    wets[0:HALO, :] = edge[4 * pieces : 4 * pieces + HALO, :]
    wets[HALO + rows : total, :] = edge[4 * pieces + HALO : 4 * pieces + 2 * HALO, :]
    force[:, 0:HALO, :] = low[...]
    force[:, HALO : HALO + rows, :] = imported[...]
    force[:, HALO + rows : total, :] = high[...]
    for field in range(width):
        flat[pl.ds(field * rows, rows), :] = imported[field]

    @pl.loop(0, rows, unroll=8)
    def _(row):
        here = pl.ds(pl.multiple_of(row * LANES, LANES), LANES)
        imported_out[:, here] = flat[pl.ds(row, width, stride=rows), :]

    def from_mixed(level, group, row):
        return mixed[pl.ds(level * total + row, GROUP), :]

    def solve(chunk, source, spread_sum, out, wide):
        for group in range(CHUNK // GROUP):
            row = pl.multiple_of(chunk * CHUNK + group * GROUP, GROUP)
            here = pl.ds(row, GROUP)
            left = keep[here, :]
            wet = wets[here, :]
            partial = []
            for level in range(levels):
                value = left * source[pl.ds(level * pitch + PAD + row, GROUP), :]
                value = value + spread_sum(level, group, row)
                if level < width:
                    value = value + force[level, here, :] * wet
                value = value * inv[level, here, :]
                if level:
                    value = value + from_up[level, here, :] * partial[-1]
                partial.append(value)
            following = partial[-1]
            out[pl.ds((levels - 1) * pitch + PAD + row, GROUP), :] = following
            for level in range(levels - 2, -1, -1):
                following = partial[level] + from_down[level, here, :] * following
                out[pl.ds(level * pitch + PAD + row, GROUP), :] = following
        for row in range(CHUNK):
            to_lanes(levels, out, wide, chunk * CHUNK + row)

    def spread(chunk, source, wide):
        by_matrix, by_gather = group_rows(chunk, chunks)
        for tile in range(GROUP):
            spread_tile(
                levels, total, wide, matrix, chunk * GROUP + tile, by_matrix + tile, mixed
            )
        here = pl.ds(by_gather, GROUP)

        def terms(which):
            return lanes[which, here, :], codes[which, here, :], coefs[which, here, :]

        spread_group(levels, total, source, by_gather, terms, mixed)

    def from_early(level, group, row):
        return early[pl.ds(level * total + row, GROUP), :]

    def from_edge(last, level, group, row):
        return edge[pl.ds((2 * last + group) * pieces + level * GROUP, GROUP), :]

    solve(0, column, functools.partial(from_edge, 0), cells, wide)

    @pl.loop(1, chunks - 1)
    def _(chunk):
        solve(chunk, column, from_early, cells, wide)

    solve(chunks - 1, column, functools.partial(from_edge, 1), cells, wide)
    for copy in late_copies:
        copy.wait()

    @pl.loop(1, STEPS)
    def _(step):
        for chunk in range(chunks):
            spread(jnp.int32(chunk), cells, wide)
        for chunk in range(chunks):
            solve(chunk, cells, from_mixed, cells, wide)

    @pl.loop(0, rows, unroll=8)
    def _(row):
        here = pl.ds(pl.multiple_of(row * LANES, LANES), LANES)
        for level in range(0, levels, 8):
            at = level * pitch + PAD + HALO + row
            state_out[level : level + 8, here] = cells[pl.ds(at, 8, stride=pitch), :]


def interval(late, early, column, edge, inv, *rest):
    levels, total = inv.shape[0], inv.shape[1]
    pitch = column.shape[0] // levels
    width, rows = rest[-3].shape[0], rest[-3].shape[1]
    operands = (early, column, edge, inv, *rest)
    late = [pltpu.with_memory_space_constraint(part, pltpu.HBM) for part in late]
    return pl.pallas_call(
        functools.partial(interval_kernel, width),
        out_shape=[
            jax.ShapeDtypeStruct((levels, rows * LANES), F32),
            jax.ShapeDtypeStruct((width, rows * LANES), F32),
        ],
        in_specs=[pl.BlockSpec(memory_space=pltpu.VMEM)] * len(operands)
        + [pl.BlockSpec(memory_space=pltpu.HBM)] * len(late),
        out_specs=[pl.BlockSpec(memory_space=pltpu.VMEM)] * 2,
        scratch_shapes=[
            pltpu.VMEM(column.shape, F32),
            pltpu.VMEM((levels * total, LANES), F32),
            pltpu.VMEM((2 * levels, pitch * LANES), BF16),
            pltpu.VMEM((width, total, LANES), F32),
            pltpu.VMEM((width * rows, LANES), F32),
            pltpu.VMEM((total, LANES), F32),
            pltpu.SemaphoreType.DMA((len(late),)),
            *[pltpu.VMEM(part.shape, part.dtype) for part in late],
        ],
        compiler_params=pltpu.CompilerParams(vmem_limit_bytes=24 * MIB),
        name="interval",
    )(*operands, *late)


def local(
    state,
    export_fields,
    remap_weights,
    routes,
    target_block,
    source_block,
    wet_mask,
    edge_coeff,
    edge_offset,
    vert_coeff,
):
    owners = lax.axis_size("dom")
    comps = lax.axis_size("comp")
    cells = state.shape[2]
    block_count = remap_weights.shape[1]
    capacity = max(2, 2 * block_count // owners)
    width = export_fields.shape[1]
    rows = cells // LANES
    me = lax.axis_index("dom").astype(jnp.int32)[None]
    coef = edge_coeff[0].reshape(-1, rows, LANES)
    offset = edge_offset[0].reshape(-1, rows, LANES)
    vert = vert_coeff[0].reshape(-1, rows, LANES)
    wet = wet_mask.reshape(rows, LANES)

    values, low, high = remap(
        routes[0, :, 0],
        target_block[0],
        source_block[0],
        me,
        export_fields[0],
        remap_weights[0],
        state[0],
        (coef, offset, vert, wet),
        owners,
        capacity,
    )
    values = lax.all_to_all(values, "dom", split_axis=0, concat_axis=0, tiled=True)

    forward = [(i, (i + 1) % owners) for i in range(owners)]
    backward = [(target, source) for source, target in forward]
    low = lax.ppermute(low, "dom", forward)
    high = lax.ppermute(high, "dom", backward)
    built = build(state[0], coef, offset, wet)
    values, built, low, high = lax.optimization_barrier((values, built, low, high))
    early, *matrix = built
    early = pltpu.with_memory_space_constraint(early, pltpu.VMEM)

    pitch = capacity * width + 8
    summed, first_rows, last_rows = assemble(
        values.reshape(owners * pitch, LANES), owners, capacity, width, rows
    )

    def across(value, shift):
        pairs = [
            (comp * owners + dom, (comp + 1) % comps * owners + (dom + shift) % owners)
            for comp in range(comps)
            for dom in range(owners)
        ]
        return lax.ppermute(value, ("comp", "dom"), pairs)

    imported = across(summed, 0)
    from_low = across(last_rows, 1)
    from_high = across(first_rows, -1)
    prepared = prepare(state[0], coef, offset, vert, low, high, matrix[:EARLY])
    new_state, imported = interval(
        matrix[EARLY:], early, *prepared, imported, from_low, from_high
    )
    return (new_state[None], imported[None])


def solution(mesh):
    placed = (
        P("comp", None, "dom"),
        P("comp", None, "dom"),
        P("comp", "dom", None, None),
        P("comp", "dom", None),
        P("comp", "dom"),
        P("comp", "dom"),
        P("comp", "dom"),
        P("comp", None, "dom"),
        P("comp", None, "dom"),
        P("comp", None, "dom"),
    )
    return jax.shard_map(
        local,
        mesh=mesh,
        in_specs=placed,
        out_specs=(P("comp", None, "dom"), P("comp", None, "dom")),
        check_vma=False,
    )
```

```python
import functools

import jax
import jax.numpy as jnp
from jax import lax
from jax.experimental import pallas as pl
from jax.experimental.pallas import tpu as pltpu
from jax.sharding import PartitionSpec as P

NB = 6
RIM = 256
STEPS = 4
LANES = 128
REACH = RIM // LANES
WINDOW = 2 * REACH + 1
EARLY = WINDOW - 1
HALO = STEPS * REACH
PAD = 8
MIB = 2**20
GROUP = 8
CHUNK = 2 * GROUP

force_scale = 0.5

F32 = jnp.float32
BF16 = jnp.bfloat16


def split(value):
    high = value.astype(BF16)
    return high, (value - high.astype(F32)).astype(BF16)


def remap_kernel(
    owners, capacity, routes, target, source, me, fields_far, weights_far, *refs
):
    far, (out, low, high, fields, weights, *refs) = refs[:5], refs[5:]
    near, (counts, marks, filled, loaded) = refs[:10], refs[10:]
    block_count = weights.shape[0]
    per_step = 16
    width = fields.shape[0]
    levels, cells = far[0].shape
    rows = cells // LANES
    edge = HALO * LANES
    lane = lax.broadcasted_iota(jnp.int32, (1, LANES), 1)
    label_row = capacity * width

    def chunk_copy(step):
        here = pl.ds(step * per_step, per_step)
        return pltpu.make_async_copy(weights_far.at[here], weights.at[here], loaded.at[step])

    fields_copy = pltpu.make_async_copy(fields_far, fields, filled.at[10])
    fields_copy.start()
    for step in range(block_count // per_step):
        chunk_copy(step).start()
    edge_copies = []
    for index, part in enumerate(far):
        for side in range(2):
            if index == 0:
                piece = part.at[:, pl.ds((0 if side else cells - edge), edge)]
            elif len(part.shape) == 3:
                piece = part.at[:, pl.ds((0 if side else rows - HALO), HALO), :]
            else:
                piece = part.at[pl.ds((0 if side else rows - HALO), HALO), :]
            at = 2 * index + side
            edge_copies.append(pltpu.make_async_copy(piece, near[at], filled.at[at]))
            edge_copies[-1].start()

    out[...] = jnp.zeros_like(out)
    marks[...] = jnp.zeros_like(marks)
    for owner in range(owners):
        counts[owner] = 0
    fields_copy.wait()

    @pl.loop(0, block_count // per_step)
    def _(step):
        chunk_copy(step).wait()
        remap_blocks(
            capacity, step * per_step, per_step, routes, target, source, me, fields, weights,
            out, counts, marks, lane,
        )

    for owner in range(owners):
        out[owner, label_row : label_row + 1, :] = marks[owner : owner + 1, :]
    for copy in edge_copies:
        copy.wait()
    for side, pack in ((0, low), (1, high)):
        state, coef, offset, vert, wet = near[side::2]
        for row in range(HALO):
            for level in range(0, levels, 8):
                tile = state[level : level + 8, row * LANES : (row + 1) * LANES]
                pack[pl.ds(level * HALO + row, 8, stride=HALO), :] = tile
        at = levels * HALO
        for part in (coef, offset, vert):
            for index in range(part.shape[0]):
                pack[at : at + HALO, :] = part[index].astype(F32)
                at += HALO
        pack[at : at + HALO, :] = wet[...].astype(F32)


def remap_blocks(
    capacity, first, count, routes, target, source, me, fields, weights, out, counts, marks, lane
):
    width = fields.shape[0]
    for index in range(count):
        block = first + index
        owner = routes[block]
        rank = counts[owner]
        counts[owner] = rank + 1
        start = pl.multiple_of(source[block] * LANES, LANES)
        picked_high, picked_low = split(fields[:, pl.ds(start, LANES)])
        picked = jnp.concatenate([picked_high, picked_low], axis=0)
        both = jnp.concatenate(split(weights[block]), axis=1)
        product = jnp.dot(picked, both, preferred_element_type=F32)
        product = product[:, :LANES] + product[:, LANES:]
        value = product[:width] + product[width:]
        row = pl.multiple_of(rank * width, width)
        out[owner, pl.ds(row, width), :] = value
        slot = lax.rem(me[0] * capacity + rank, LANES)
        marks[pl.ds(owner, 1), :] = jnp.where(
            lane == slot, (target[block] + 1).astype(F32), marks[pl.ds(owner, 1), :]
        )


def remap(routes, target, source, me, fields, weights, state, parts, owners, capacity):
    block_count = weights.shape[0]
    width = fields.shape[0]
    levels = state.shape[0]
    scratch = [pltpu.VMEM((levels, HALO * LANES), F32)] * 2
    pack_rows = levels * HALO
    for part in parts:
        count = part.shape[0] if part.ndim == 3 else 1
        scratch += [pltpu.VMEM((*part.shape[:-2], HALO, LANES), part.dtype)] * 2
        pack_rows += count * HALO
    slots = (owners, capacity * width + 8, LANES)
    scalar = pl.BlockSpec(memory_space=pltpu.SMEM)
    far = pl.BlockSpec(memory_space=pltpu.HBM)
    near = pl.BlockSpec(memory_space=pltpu.VMEM)
    return pl.pallas_call(
        functools.partial(remap_kernel, owners, capacity),
        in_specs=[scalar] * 4 + [far] * 7,
        out_specs=[near] * 3,
        out_shape=[
            jax.ShapeDtypeStruct(slots, F32),
            jax.ShapeDtypeStruct((pack_rows, LANES), F32),
            jax.ShapeDtypeStruct((pack_rows, LANES), F32),
        ],
        scratch_shapes=[
            pltpu.VMEM(fields.shape, F32),
            pltpu.VMEM(weights.shape, F32),
            *scratch,
            pltpu.SMEM((owners,), jnp.int32),
            pltpu.VMEM((owners, LANES), F32),
            pltpu.SemaphoreType.DMA((11,)),
            pltpu.SemaphoreType.DMA((block_count // 16,)),
        ],
        compiler_params=pltpu.CompilerParams(vmem_limit_bytes=60 * MIB),
        name="remap",
    )(routes, target, source, me, fields, weights, state, *parts)


def assemble_kernel(owners, capacity, width, slots, out, low, high, hot, values):
    rows = out.shape[1]
    count = owners * capacity
    per_row = LANES // capacity
    size = capacity * width
    pitch = size + 8
    block = lax.broadcasted_iota(jnp.int32, (rows, LANES), 0) + 1
    for sender in range(owners):
        values[sender * size : (sender + 1) * size, :] = slots[
            sender * pitch : sender * pitch + size, :
        ]
    for half in range(count // LANES):
        label = None
        for sender in range(half * per_row, (half + 1) * per_row):
            row = slots[sender * pitch + size : sender * pitch + size + 1, :]
            label = row if label is None else label + row
        label = jnp.broadcast_to(label.astype(jnp.int32), (rows, LANES))
        hot[:, half * LANES : (half + 1) * LANES] = (label == block).astype(F32).astype(BF16)
    picks = hot[...]
    for field in range(width):
        value_high, value_low = split(values[pl.ds(field, count, stride=width), :])
        both = jnp.concatenate([value_high, value_low], axis=1)
        total = jnp.dot(picks, both, preferred_element_type=F32)
        total = total[:, :LANES] + total[:, LANES:]
        out[field] = total
        low[field] = total[:HALO]
        high[field] = total[rows - HALO :]


def assemble(slots, owners, capacity, width, rows):
    return pl.pallas_call(
        functools.partial(assemble_kernel, owners, capacity, width),
        out_shape=[
            jax.ShapeDtypeStruct((width, rows, LANES), F32),
            jax.ShapeDtypeStruct((width, HALO, LANES), F32),
            jax.ShapeDtypeStruct((width, HALO, LANES), F32),
        ],
        scratch_shapes=[
            pltpu.VMEM((rows, owners * capacity), BF16),
            pltpu.VMEM((owners * capacity * width, LANES), F32),
        ],
        compiler_params=pltpu.CompilerParams(vmem_limit_bytes=12 * MIB),
        name="assemble",
    )(slots)


def lane_pick(value, index):
    return jnp.take_along_axis(value, index, axis=1, mode="promise_in_bounds")


def group_rows(chunk, chunks):
    base = chunk * CHUNK
    late = (chunk > chunks // 2).astype(jnp.int32) * GROUP
    return pl.multiple_of(base + GROUP - late, GROUP), pl.multiple_of(base + late, GROUP)


def to_lanes(levels, column, wide, row):
    pitch = column.shape[0] // levels
    here = pl.ds(pl.multiple_of((row + PAD) * LANES, LANES), LANES)
    tiles = [
        column[pl.ds(level * pitch + PAD + row, 8, stride=pitch), :]
        for level in range(0, levels, 8)
    ]
    high, low = split(jnp.concatenate(tiles, axis=0))
    wide[0:levels, here] = high
    wide[levels : 2 * levels, here] = low


def spread_tile(levels, total, wide, matrix, entry, row, mix):
    at = pl.multiple_of((row + PAD - REACH) * LANES, LANES)
    got = jnp.dot(
        wide[:, pl.ds(at, WINDOW * LANES)],
        jnp.concatenate([part[entry] for part in matrix], axis=0),
        preferred_element_type=F32,
    )
    got = got[:, :LANES] + got[:, LANES:]
    got = got[:levels] + got[levels:]
    for level in range(0, levels, 8):
        mix[pl.ds(level * total + row, 8, stride=total), :] = got[level : level + 8]


def spread_group(levels, total, column, row, terms, mix, out=None, step=None):
    pitch = column.shape[0] // levels
    right = [None] * levels
    for which in range(NB):
        index, code, factor = terms(which)
        for level in range(levels):
            found = None
            for reach in range(WINDOW):
                at = level * pitch + PAD - REACH + reach + row
                picked = lane_pick(column[pl.ds(at, GROUP), :], index)
                found = picked if found is None else jnp.where(code == reach, picked, found)
            found = factor * found
            right[level] = found if which == 0 else right[level] + found
    out, step = (row, total) if out is None else (out, step)
    for level in range(levels):
        mix[pl.ds(level * step + out, GROUP), :] = right[level]


def edge_row(index, total):
    far = (index >= 2).astype(jnp.int32)
    return pl.multiple_of(index * GROUP + far * (total - 4 * GROUP), GROUP)


def spots_of(offset):
    return offset + lax.broadcasted_iota(jnp.int32, offset.shape, offset.ndim - 1) + RIM


def lane_of(spot):
    return jnp.bitwise_and(spot, LANES - 1)


def code_of(spot):
    return lax.shift_right_logical(spot, LANES.bit_length() - 1)


def state_rows(state, column, row):
    levels = state.shape[0]
    pitch = column.shape[0] // levels
    here = pl.ds(pl.multiple_of(row * LANES, LANES), LANES)
    for level in range(0, levels, 8):
        at = level * pitch + PAD + HALO + row
        column[pl.ds(at, 8, stride=pitch), :] = state[level : level + 8, here]


def build_kernel(state, coef, offset, wet, mix, *refs):
    matrix, (column, wide, spots, highs, lows) = refs[:WINDOW], refs[WINDOW:]
    chunk = pl.program_id(0)
    chunks = pl.num_programs(0)
    levels = state.shape[0]
    rows = state.shape[1] // LANES
    total = rows + 2 * HALO

    @pl.when(chunk == 0)
    def _():
        @pl.loop(0, rows, unroll=8)
        def _(row):
            state_rows(state, column, row)

        @pl.loop(0, rows, unroll=8)
        def _(row):
            to_lanes(levels, column, wide, row + HALO)

        mix[pl.ds(levels * total + HALO, rows), :] = wet[...].astype(F32) * force_scale

    by_matrix, by_gather = group_rows(chunk, chunks)
    here = pl.ds(pl.multiple_of(by_matrix - HALO, GROUP), GROUP)
    spot = [spots_of(offset[which, here, :]) for which in range(NB)]
    factor = [coef[which, here, :] for which in range(NB)]
    for which in range(NB):
        spots[which] = spot[which]
        joint = factor[which]
        for other in range(NB):
            if other != which:
                joint = joint + jnp.where(spot[other] == spot[which], factor[other], 0.0)
        high = joint.astype(BF16).astype(F32)
        highs[which] = high
        lows[which] = joint - high

    inside = (chunk > 0) & (chunk < chunks - 1)
    near = pl.ds(pl.multiple_of(jnp.where(inside, by_gather - HALO, 0), GROUP), GROUP)

    def terms(which):
        spot = spots_of(offset[which, near, :])
        return lane_of(spot), code_of(spot), coef[which, near, :]

    spread_group(levels, total, column, by_gather, terms, mix)

    small = jnp.int16

    @pl.loop(0, GROUP, unroll=8)
    def _(tile):
        def wide_row(ref, kind):
            return [
                jnp.broadcast_to(ref[which, pl.ds(tile, 1), :], (16, LANES)).astype(kind)
                for which in range(NB)
            ]

        spot_rows, high_rows, low_rows = (
            wide_row(spots, small),
            wide_row(highs, BF16),
            wide_row(lows, BF16),
        )
        count = lax.broadcasted_iota(jnp.int32, (16, LANES), 0).astype(small)
        for first in range(0, WINDOW * LANES, 16):
            key = count + small(first)
            by_high = jnp.zeros((16, LANES), BF16)
            by_low = jnp.zeros((16, LANES), BF16)
            for which in range(NB):
                hit = spot_rows[which] == key
                by_high = jnp.where(hit, high_rows[which], by_high)
                by_low = jnp.where(hit, low_rows[which], by_low)
            part, at = matrix[first // LANES], first % LANES
            part[tile, at : at + 16, 0:LANES] = by_high
            part[tile, at : at + 16, LANES : 2 * LANES] = by_low

    for tile in range(GROUP):
        spread_tile(levels, total, wide, matrix, tile, by_matrix + tile, mix)


def build(state, coef, offset, wet):
    levels, cells = state.shape
    rows = cells // LANES
    total = rows + 2 * HALO
    pitch = total + 2 * PAD
    chunks = total // CHUNK
    span = WINDOW * LANES
    return pl.pallas_call(
        build_kernel,
        grid=(chunks,),
        in_specs=[
            pl.BlockSpec(state.shape, lambda i: (0, 0)),
            pl.BlockSpec(coef.shape, lambda i: (0, 0, 0)),
            pl.BlockSpec(offset.shape, lambda i: (0, 0, 0)),
            pl.BlockSpec(wet.shape, lambda i: (0, 0)),
        ],
        out_specs=[
            pl.BlockSpec(((levels + 1) * total, LANES), lambda i: (0, 0)),
            *[pl.BlockSpec((GROUP, LANES, 2 * LANES), lambda i: (i, 0, 0))] * WINDOW,
        ],
        out_shape=[
            jax.ShapeDtypeStruct(((levels + 1) * total, LANES), F32),
            *[jax.ShapeDtypeStruct((chunks * GROUP, LANES, 2 * LANES), BF16)] * WINDOW,
        ],
        scratch_shapes=[
            pltpu.VMEM((levels * pitch, LANES), F32),
            pltpu.VMEM((2 * levels, pitch * LANES), BF16),
            pltpu.VMEM((NB, GROUP, LANES), jnp.int32),
            pltpu.VMEM((NB, GROUP, LANES), F32),
            pltpu.VMEM((NB, GROUP, LANES), F32),
        ],
        compiler_params=pltpu.CompilerParams(vmem_limit_bytes=56 * MIB),
        cost_estimate=pl.CostEstimate(
            flops=2 * chunks * GROUP * 2 * levels * span * 2 * LANES,
            bytes_accessed=80 * MIB,
            transcendentals=0,
        ),
        name="build",
    )(state, coef, offset, wet)


def prepare_kernel(
    state, coef, offset, vert, low_far, high_far, *refs
):
    far, (column, edge, inv, from_up, from_down, lanes, codes, coefs, keep, *refs) = (
        refs[:EARLY],
        refs[EARLY:],
    )
    matrix, (verts, low, high, packed, copied) = refs[:EARLY], refs[EARLY:]
    pack_copies = [
        pltpu.make_async_copy(source, target, packed.at[index])
        for index, (source, target) in enumerate(((low_far, low), (high_far, high)))
    ]
    matrix_copies = [
        pltpu.make_async_copy(far[reach], matrix[reach], copied.at[reach])
        for reach in range(EARLY)
    ]
    for copy in pack_copies:
        copy.start()
    levels = state.shape[0]
    rows = state.shape[1] // LANES
    total = rows + 2 * HALO
    pitch = column.shape[0] // levels
    inner = levels - 1
    pieces = levels * GROUP

    main = slice(HALO, HALO + rows)
    coefs[:, main, :] = coef[...]
    lanes[:, main, :] = offset[...]
    verts[:, main, :] = vert[...]

    @pl.loop(0, rows, unroll=8)
    def _(row):
        state_rows(state, column, row)

    for copy in pack_copies:
        copy.wait()
    for copy in matrix_copies:
        copy.start()
    for pack, first in ((low, 0), (high, total - HALO)):
        for level in range(levels):
            at = level * pitch + PAD + first
            column[at : at + HALO, :] = pack[level * HALO : (level + 1) * HALO, :]
        here = slice(first, first + HALO)
        at = levels * HALO
        for out, count in ((coefs, NB), (lanes, NB), (verts, inner)):
            for index in range(count):
                out[index, here, :] = pack[at : at + HALO, :].astype(out.dtype)
                at += HALO
        to = 4 * pieces + (0 if first == 0 else HALO)
        edge[to : to + HALO, :] = pack[at : at + HALO, :] * force_scale

    @pl.loop(0, total // GROUP)
    def _(group):
        here = pl.ds(pl.multiple_of(group * GROUP, GROUP), GROUP)
        left = 1.0
        for which in range(NB):
            spot = spots_of(lanes[which, here, :])
            lanes[which, here, :] = lane_of(spot)
            codes[which, here, :] = code_of(spot)
            left = left - coefs[which, here, :]
        keep[here, :] = left
        upper = jnp.zeros((GROUP, LANES), F32)
        carried = jnp.zeros((GROUP, LANES), F32)
        for level in range(levels):
            lower = verts[level, here, :] if level < inner else jnp.zeros((GROUP, LANES), F32)
            pivot = (1.0 + upper + lower) - upper * carried
            inverse = 1.0 / pivot
            carried = lower * inverse
            inv[level, here, :] = inverse
            from_up[level, here, :] = upper * inverse
            from_down[level, here, :] = carried
            upper = lower

    @pl.loop(0, 4)
    def _(index):
        row = edge_row(index, total)
        here = pl.ds(row, GROUP)

        def terms(which):
            return lanes[which, here, :], codes[which, here, :], coefs[which, here, :]

        spread_group(levels, total, column, row, terms, edge, index * pieces, GROUP)

    for copy in matrix_copies:
        copy.wait()


def prepare(state, coef, offset, vert, low, high, matrix):
    levels, cells = state.shape
    rows = cells // LANES
    total = rows + 2 * HALO
    pitch = total + 2 * PAD
    level_shape = pltpu.VMEM((levels, total, LANES), F32)
    index_shape = pltpu.VMEM((NB, total, LANES), jnp.int32)
    near = pl.BlockSpec(memory_space=pltpu.VMEM)
    far = pl.BlockSpec(memory_space=pltpu.HBM)
    low, high, *matrix = [
        pltpu.with_memory_space_constraint(part, pltpu.HBM) for part in (low, high, *matrix)
    ]
    return pl.pallas_call(
        prepare_kernel,
        out_shape=[
            pltpu.VMEM((levels * pitch, LANES), F32),
            pltpu.VMEM((4 * levels * GROUP + 2 * HALO, LANES), F32),
            level_shape,
            level_shape,
            level_shape,
            index_shape,
            index_shape,
            pltpu.VMEM((NB, total, LANES), F32),
            pltpu.VMEM((total, LANES), F32),
            *[pltpu.VMEM(part.shape, part.dtype) for part in matrix],
        ],
        in_specs=[near] * 4 + [far] * (2 + EARLY),
        out_specs=[near] * (9 + EARLY),
        scratch_shapes=[
            pltpu.VMEM((levels - 1, total, LANES), F32),
            pltpu.VMEM(low.shape, F32),
            pltpu.VMEM(high.shape, F32),
            pltpu.SemaphoreType.DMA((2,)),
            pltpu.SemaphoreType.DMA((EARLY,)),
        ],
        compiler_params=pltpu.CompilerParams(vmem_limit_bytes=24 * MIB),
        cost_estimate=pl.CostEstimate(flops=0, bytes_accessed=16 * MIB, transcendentals=0),
        name="prepare",
    )(state, coef, offset, vert, low, high, *matrix)


def interval_kernel(
    width, early, column, edge, inv, from_up, from_down, lanes, codes, coefs, keep, *refs
):
    matrix, refs = refs[:EARLY], refs[EARLY:]
    imported, low, high, refs = *refs[:3], refs[3:]
    late_far, (state_out, imported_out, *refs) = refs[: WINDOW - EARLY], refs[WINDOW - EARLY :]
    cells, mixed, wide, force, flat, wets, copied, *late = refs
    matrix = (*matrix, *late)
    late_copies = [
        pltpu.make_async_copy(source, part, copied.at[index])
        for index, (source, part) in enumerate(zip(late_far, late))
    ]
    for copy in late_copies:
        copy.start()
    levels, total = inv.shape[0], inv.shape[1]
    rows = total - 2 * HALO
    pitch = column.shape[0] // levels
    chunks = total // CHUNK

    pieces = levels * GROUP
    wets[...] = early[levels * total : (levels + 1) * total, :]
    wets[0:HALO, :] = edge[4 * pieces : 4 * pieces + HALO, :]
    wets[HALO + rows : total, :] = edge[4 * pieces + HALO : 4 * pieces + 2 * HALO, :]
    force[:, 0:HALO, :] = low[...]
    force[:, HALO : HALO + rows, :] = imported[...]
    force[:, HALO + rows : total, :] = high[...]
    for field in range(width):
        flat[pl.ds(field * rows, rows), :] = imported[field]

    @pl.loop(0, rows, unroll=8)
    def _(row):
        here = pl.ds(pl.multiple_of(row * LANES, LANES), LANES)
        imported_out[:, here] = flat[pl.ds(row, width, stride=rows), :]

    def from_mixed(level, group, row):
        return mixed[pl.ds(level * total + row, GROUP), :]

    def solve(chunk, source, spread_sum, out, wide, groups=(0, 1)):
        for group in groups:
            row = pl.multiple_of(chunk * CHUNK + group * GROUP, GROUP)
            here = pl.ds(row, GROUP)
            left = keep[here, :]
            wet = wets[here, :]
            partial = []
            for level in range(levels):
                value = left * source[pl.ds(level * pitch + PAD + row, GROUP), :]
                value = value + spread_sum(level, group, row)
                if level < width:
                    value = value + force[level, here, :] * wet
                value = value * inv[level, here, :]
                if level:
                    value = value + from_up[level, here, :] * partial[-1]
                partial.append(value)
            following = partial[-1]
            out[pl.ds((levels - 1) * pitch + PAD + row, GROUP), :] = following
            for level in range(levels - 2, -1, -1):
                following = partial[level] + from_down[level, here, :] * following
                out[pl.ds(level * pitch + PAD + row, GROUP), :] = following
        for row in range(CHUNK if wide is not None else 0):
            to_lanes(levels, out, wide, chunk * CHUNK + row)

    def spread(chunk, source, wide, gathers=True):
        by_matrix, by_gather = group_rows(chunk, chunks)
        for tile in range(GROUP):
            spread_tile(
                levels, total, wide, matrix, chunk * GROUP + tile, by_matrix + tile, mixed
            )
        if not gathers:
            return
        here = pl.ds(by_gather, GROUP)

        def terms(which):
            return lanes[which, here, :], codes[which, here, :], coefs[which, here, :]

        spread_group(levels, total, source, by_gather, terms, mixed)

    def from_early(level, group, row):
        return early[pl.ds(level * total + row, GROUP), :]

    def from_edge(last, level, group, row):
        return edge[pl.ds((2 * last + group) * pieces + level * GROUP, GROUP), :]

    solve(0, column, functools.partial(from_edge, 0), cells, wide)

    @pl.loop(1, chunks - 1)
    def _(chunk):
        solve(chunk, column, from_early, cells, wide)

    solve(chunks - 1, column, functools.partial(from_edge, 1), cells, wide)
    for copy in late_copies:
        copy.wait()

    @pl.loop(1, STEPS - 1)
    def _(step):
        for chunk in range(chunks):
            spread(jnp.int32(chunk), cells, wide)
        for chunk in range(chunks):
            solve(chunk, cells, from_mixed, cells, wide)

    for chunk in range(chunks):
        spread(jnp.int32(chunk), cells, wide, 0 < chunk < chunks - 1)
    for chunk in range(chunks):
        groups = (1,) if chunk == 0 else (0,) if chunk == chunks - 1 else (0, 1)
        solve(chunk, cells, from_mixed, cells, None, groups)

    @pl.loop(0, rows, unroll=8)
    def _(row):
        here = pl.ds(pl.multiple_of(row * LANES, LANES), LANES)
        for level in range(0, levels, 8):
            at = level * pitch + PAD + HALO + row
            state_out[level : level + 8, here] = cells[pl.ds(at, 8, stride=pitch), :]


def interval(late, early, column, edge, inv, *rest):
    levels, total = inv.shape[0], inv.shape[1]
    pitch = column.shape[0] // levels
    width, rows = rest[-3].shape[0], rest[-3].shape[1]
    operands = (early, column, edge, inv, *rest)
    late = [pltpu.with_memory_space_constraint(part, pltpu.HBM) for part in late]
    return pl.pallas_call(
        functools.partial(interval_kernel, width),
        out_shape=[
            jax.ShapeDtypeStruct((levels, rows * LANES), F32),
            jax.ShapeDtypeStruct((width, rows * LANES), F32),
        ],
        in_specs=[pl.BlockSpec(memory_space=pltpu.VMEM)] * len(operands)
        + [pl.BlockSpec(memory_space=pltpu.HBM)] * len(late),
        out_specs=[pl.BlockSpec(memory_space=pltpu.VMEM)] * 2,
        scratch_shapes=[
            pltpu.VMEM(column.shape, F32),
            pltpu.VMEM((levels * total, LANES), F32),
            pltpu.VMEM((2 * levels, pitch * LANES), BF16),
            pltpu.VMEM((width, total, LANES), F32),
            pltpu.VMEM((width * rows, LANES), F32),
            pltpu.VMEM((total, LANES), F32),
            pltpu.SemaphoreType.DMA((len(late),)),
            *[pltpu.VMEM(part.shape, part.dtype) for part in late],
        ],
        compiler_params=pltpu.CompilerParams(vmem_limit_bytes=24 * MIB),
        name="interval",
    )(*operands, *late)


def local(
    state,
    export_fields,
    remap_weights,
    routes,
    target_block,
    source_block,
    wet_mask,
    edge_coeff,
    edge_offset,
    vert_coeff,
):
    owners = lax.axis_size("dom")
    comps = lax.axis_size("comp")
    cells = state.shape[2]
    block_count = remap_weights.shape[1]
    capacity = max(2, 2 * block_count // owners)
    width = export_fields.shape[1]
    rows = cells // LANES
    me = lax.axis_index("dom").astype(jnp.int32)[None]
    coef = edge_coeff[0].reshape(-1, rows, LANES)
    offset = edge_offset[0].reshape(-1, rows, LANES)
    vert = vert_coeff[0].reshape(-1, rows, LANES)
    wet = wet_mask.reshape(rows, LANES)

    values, low, high = remap(
        routes[0, :, 0],
        target_block[0],
        source_block[0],
        me,
        export_fields[0],
        remap_weights[0],
        state[0],
        (coef, offset, vert, wet),
        owners,
        capacity,
    )
    values = lax.all_to_all(values, "dom", split_axis=0, concat_axis=0, tiled=True)

    forward = [(i, (i + 1) % owners) for i in range(owners)]
    backward = [(target, source) for source, target in forward]
    low = lax.ppermute(low, "dom", forward)
    high = lax.ppermute(high, "dom", backward)
    built = build(state[0], coef, offset, wet)
    values, built, low, high = lax.optimization_barrier((values, built, low, high))
    early, *matrix = built
    early = pltpu.with_memory_space_constraint(early, pltpu.VMEM)

    pitch = capacity * width + 8
    summed, first_rows, last_rows = assemble(
        values.reshape(owners * pitch, LANES), owners, capacity, width, rows
    )

    def across(value, shift):
        pairs = [
            (comp * owners + dom, (comp + 1) % comps * owners + (dom + shift) % owners)
            for comp in range(comps)
            for dom in range(owners)
        ]
        return lax.ppermute(value, ("comp", "dom"), pairs)

    imported = across(summed, 0)
    from_low = across(last_rows, 1)
    from_high = across(first_rows, -1)
    prepared = prepare(state[0], coef, offset, vert, low, high, matrix[:EARLY])
    new_state, imported = interval(
        matrix[EARLY:], early, *prepared, imported, from_low, from_high
    )
    return (new_state[None], imported[None])


def solution(mesh):
    placed = (
        P("comp", None, "dom"),
        P("comp", None, "dom"),
        P("comp", "dom", None, None),
        P("comp", "dom", None),
        P("comp", "dom"),
        P("comp", "dom"),
        P("comp", "dom"),
        P("comp", None, "dom"),
        P("comp", None, "dom"),
        P("comp", None, "dom"),
    )
    return jax.shard_map(
        local,
        mesh=mesh,
        in_specs=placed,
        out_specs=(P("comp", None, "dom"), P("comp", None, "dom")),
        check_vma=False,
    )
```

```python
import functools

import jax
import jax.numpy as jnp
from jax import lax
from jax.experimental import pallas as pl
from jax.experimental.pallas import tpu as pltpu
from jax.sharding import PartitionSpec as P

NB = 6
RIM = 256
STEPS = 4
LANES = 128
REACH = RIM // LANES
WINDOW = 2 * REACH + 1
EARLY = WINDOW - 1
HALO = STEPS * REACH
PAD = 8
MIB = 2**20
GROUP = 8
CHUNK = 2 * GROUP

force_scale = 0.5

F32 = jnp.float32
BF16 = jnp.bfloat16


def split(value):
    high = value.astype(BF16)
    return high, (value - high.astype(F32)).astype(BF16)


def remap_kernel(
    owners, capacity, routes, target, source, me, fields_far, weights_far, *refs
):
    far, (out, low, high, fields, weights, *refs) = refs[:5], refs[5:]
    near, (counts, marks, filled, loaded) = refs[:10], refs[10:]
    block_count = weights.shape[0]
    per_step = 16
    width = fields.shape[0]
    levels, cells = far[0].shape
    rows = cells // LANES
    edge = HALO * LANES
    lane = lax.broadcasted_iota(jnp.int32, (1, LANES), 1)
    label_row = capacity * width

    def chunk_copy(step):
        here = pl.ds(step * per_step, per_step)
        return pltpu.make_async_copy(weights_far.at[here], weights.at[here], loaded.at[step])

    fields_copy = pltpu.make_async_copy(fields_far, fields, filled.at[10])
    fields_copy.start()
    for step in range(block_count // per_step):
        chunk_copy(step).start()
    edge_copies = []
    for index, part in enumerate(far):
        for side in range(2):
            if index == 0:
                piece = part.at[:, pl.ds((0 if side else cells - edge), edge)]
            elif len(part.shape) == 3:
                piece = part.at[:, pl.ds((0 if side else rows - HALO), HALO), :]
            else:
                piece = part.at[pl.ds((0 if side else rows - HALO), HALO), :]
            at = 2 * index + side
            edge_copies.append(pltpu.make_async_copy(piece, near[at], filled.at[at]))
            edge_copies[-1].start()

    out[...] = jnp.zeros_like(out)
    marks[...] = jnp.zeros_like(marks)
    for owner in range(owners):
        counts[owner] = 0
    fields_copy.wait()

    @pl.loop(0, block_count // per_step)
    def _(step):
        chunk_copy(step).wait()
        remap_blocks(
            capacity, step * per_step, per_step, routes, target, source, me, fields, weights,
            out, counts, marks, lane,
        )

    for owner in range(owners):
        out[owner, label_row : label_row + 1, :] = marks[owner : owner + 1, :]
    for copy in edge_copies:
        copy.wait()
    for side, pack in ((0, low), (1, high)):
        state, coef, offset, vert, wet = near[side::2]
        for row in range(HALO):
            for level in range(0, levels, 8):
                tile = state[level : level + 8, row * LANES : (row + 1) * LANES]
                pack[pl.ds(level * HALO + row, 8, stride=HALO), :] = tile
        at = levels * HALO
        for part in (coef, offset, vert):
            for index in range(part.shape[0]):
                pack[at : at + HALO, :] = part[index].astype(F32)
                at += HALO
        pack[at : at + HALO, :] = wet[...].astype(F32)


def remap_blocks(
    capacity, first, count, routes, target, source, me, fields, weights, out, counts, marks, lane
):
    width = fields.shape[0]
    for index in range(count):
        block = first + index
        owner = routes[block]
        rank = counts[owner]
        counts[owner] = rank + 1
        start = pl.multiple_of(source[block] * LANES, LANES)
        picked_high, picked_low = split(fields[:, pl.ds(start, LANES)])
        picked = jnp.concatenate([picked_high, picked_low], axis=0)
        both = jnp.concatenate(split(weights[block]), axis=1)
        product = jnp.dot(picked, both, preferred_element_type=F32)
        product = product[:, :LANES] + product[:, LANES:]
        value = product[:width] + product[width:]
        row = pl.multiple_of(rank * width, width)
        out[owner, pl.ds(row, width), :] = value
        slot = lax.rem(me[0] * capacity + rank, LANES)
        marks[pl.ds(owner, 1), :] = jnp.where(
            lane == slot, (target[block] + 1).astype(F32), marks[pl.ds(owner, 1), :]
        )


def remap(routes, target, source, me, fields, weights, state, parts, owners, capacity):
    block_count = weights.shape[0]
    width = fields.shape[0]
    levels = state.shape[0]
    scratch = [pltpu.VMEM((levels, HALO * LANES), F32)] * 2
    pack_rows = levels * HALO
    for part in parts:
        count = part.shape[0] if part.ndim == 3 else 1
        scratch += [pltpu.VMEM((*part.shape[:-2], HALO, LANES), part.dtype)] * 2
        pack_rows += count * HALO
    slots = (owners, capacity * width + 8, LANES)
    scalar = pl.BlockSpec(memory_space=pltpu.SMEM)
    far = pl.BlockSpec(memory_space=pltpu.HBM)
    near = pl.BlockSpec(memory_space=pltpu.VMEM)
    return pl.pallas_call(
        functools.partial(remap_kernel, owners, capacity),
        in_specs=[scalar] * 4 + [far] * 7,
        out_specs=[near] * 3,
        out_shape=[
            jax.ShapeDtypeStruct(slots, F32),
            jax.ShapeDtypeStruct((pack_rows, LANES), F32),
            jax.ShapeDtypeStruct((pack_rows, LANES), F32),
        ],
        scratch_shapes=[
            pltpu.VMEM(fields.shape, F32),
            pltpu.VMEM(weights.shape, F32),
            *scratch,
            pltpu.SMEM((owners,), jnp.int32),
            pltpu.VMEM((owners, LANES), F32),
            pltpu.SemaphoreType.DMA((11,)),
            pltpu.SemaphoreType.DMA((block_count // 16,)),
        ],
        compiler_params=pltpu.CompilerParams(vmem_limit_bytes=60 * MIB),
        name="remap",
    )(routes, target, source, me, fields, weights, state, *parts)


def assemble_kernel(owners, capacity, width, slots, out, low, high, hot, values):
    rows = out.shape[1]
    count = owners * capacity
    per_row = LANES // capacity
    size = capacity * width
    pitch = size + 8
    block = lax.broadcasted_iota(jnp.int32, (rows, LANES), 0) + 1
    for sender in range(owners):
        values[sender * size : (sender + 1) * size, :] = slots[
            sender * pitch : sender * pitch + size, :
        ]
    for half in range(count // LANES):
        label = None
        for sender in range(half * per_row, (half + 1) * per_row):
            row = slots[sender * pitch + size : sender * pitch + size + 1, :]
            label = row if label is None else label + row
        label = jnp.broadcast_to(label.astype(jnp.int32), (rows, LANES))
        hot[:, half * LANES : (half + 1) * LANES] = (label == block).astype(F32).astype(BF16)
    picks = hot[...]
    for field in range(width):
        value_high, value_low = split(values[pl.ds(field, count, stride=width), :])
        both = jnp.concatenate([value_high, value_low], axis=1)
        total = jnp.dot(picks, both, preferred_element_type=F32)
        total = total[:, :LANES] + total[:, LANES:]
        out[field] = total
        low[field] = total[:HALO]
        high[field] = total[rows - HALO :]


def assemble(slots, owners, capacity, width, rows):
    return pl.pallas_call(
        functools.partial(assemble_kernel, owners, capacity, width),
        out_shape=[
            jax.ShapeDtypeStruct((width, rows, LANES), F32),
            jax.ShapeDtypeStruct((width, HALO, LANES), F32),
            jax.ShapeDtypeStruct((width, HALO, LANES), F32),
        ],
        scratch_shapes=[
            pltpu.VMEM((rows, owners * capacity), BF16),
            pltpu.VMEM((owners * capacity * width, LANES), F32),
        ],
        compiler_params=pltpu.CompilerParams(vmem_limit_bytes=12 * MIB),
        name="assemble",
    )(slots)


def lane_pick(value, index):
    return jnp.take_along_axis(value, index, axis=1, mode="promise_in_bounds")


def group_rows(chunk, chunks):
    base = chunk * CHUNK
    late = (chunk > chunks // 2).astype(jnp.int32) * GROUP
    return pl.multiple_of(base + GROUP - late, GROUP), pl.multiple_of(base + late, GROUP)


def to_lanes(levels, column, wide, row):
    pitch = column.shape[0] // levels
    here = pl.ds(pl.multiple_of((row + PAD) * LANES, LANES), LANES)
    tiles = [
        column[pl.ds(level * pitch + PAD + row, 8, stride=pitch), :]
        for level in range(0, levels, 8)
    ]
    high, low = split(jnp.concatenate(tiles, axis=0))
    wide[0:levels, here] = high
    wide[levels : 2 * levels, here] = low


def spread_tile(levels, total, wide, matrix, entry, row, mix):
    at = pl.multiple_of((row + PAD - REACH) * LANES, LANES)
    got = jnp.dot(
        wide[:, pl.ds(at, WINDOW * LANES)],
        jnp.concatenate([part[entry] for part in matrix], axis=0),
        preferred_element_type=F32,
    )
    got = got[:, :LANES] + got[:, LANES:]
    got = got[:levels] + got[levels:]
    for level in range(0, levels, 8):
        mix[pl.ds(level * total + row, 8, stride=total), :] = got[level : level + 8]


def spread_group(levels, total, column, row, terms, mix, out=None, step=None):
    pitch = column.shape[0] // levels
    right = [None] * levels
    for which in range(NB):
        index, code, factor = terms(which)
        for level in range(levels):
            found = None
            for reach in range(WINDOW):
                at = level * pitch + PAD - REACH + reach + row
                picked = lane_pick(column[pl.ds(at, GROUP), :], index)
                found = picked if found is None else jnp.where(code == reach, picked, found)
            found = factor * found
            right[level] = found if which == 0 else right[level] + found
    out, step = (row, total) if out is None else (out, step)
    for level in range(levels):
        mix[pl.ds(level * step + out, GROUP), :] = right[level]


def edge_row(index, total):
    far = (index >= 2).astype(jnp.int32)
    return pl.multiple_of(index * GROUP + far * (total - 4 * GROUP), GROUP)


def spots_of(offset):
    return offset + lax.broadcasted_iota(jnp.int32, offset.shape, offset.ndim - 1) + RIM


def lane_of(spot):
    return jnp.bitwise_and(spot, LANES - 1)


def code_of(spot):
    return lax.shift_right_logical(spot, LANES.bit_length() - 1)


def state_rows(state, column, row):
    levels = state.shape[0]
    pitch = column.shape[0] // levels
    here = pl.ds(pl.multiple_of(row * LANES, LANES), LANES)
    for level in range(0, levels, 8):
        at = level * pitch + PAD + HALO + row
        column[pl.ds(at, 8, stride=pitch), :] = state[level : level + 8, here]


def build_kernel(state, coef, offset, wet, mix, *refs):
    matrix, (column, wide, spots, highs, lows) = refs[:WINDOW], refs[WINDOW:]
    chunk = pl.program_id(0)
    chunks = pl.num_programs(0)
    levels = state.shape[0]
    rows = state.shape[1] // LANES
    total = rows + 2 * HALO

    @pl.when(chunk == 0)
    def _():
        @pl.loop(0, rows, unroll=8)
        def _(row):
            state_rows(state, column, row)

        @pl.loop(0, rows, unroll=8)
        def _(row):
            to_lanes(levels, column, wide, row + HALO)

        mix[pl.ds(levels * total + HALO, rows), :] = wet[...].astype(F32) * force_scale

    by_matrix, by_gather = group_rows(chunk, chunks)
    here = pl.ds(pl.multiple_of(by_matrix - HALO, GROUP), GROUP)
    spot = [spots_of(offset[which, here, :]) for which in range(NB)]
    factor = [coef[which, here, :] for which in range(NB)]
    for which in range(NB):
        spots[which] = spot[which]
        joint = factor[which]
        for other in range(NB):
            if other != which:
                joint = joint + jnp.where(spot[other] == spot[which], factor[other], 0.0)
        high = joint.astype(BF16).astype(F32)
        highs[which] = high
        lows[which] = joint - high

    inside = (chunk > 0) & (chunk < chunks - 1)
    near = pl.ds(pl.multiple_of(jnp.where(inside, by_gather - HALO, 0), GROUP), GROUP)

    def terms(which):
        spot = spots_of(offset[which, near, :])
        return lane_of(spot), code_of(spot), coef[which, near, :]

    spread_group(levels, total, column, by_gather, terms, mix)

    small = jnp.int16

    @pl.loop(0, GROUP, unroll=8)
    def _(tile):
        def wide_row(ref, kind):
            return [
                jnp.broadcast_to(ref[which, pl.ds(tile, 1), :], (16, LANES)).astype(kind)
                for which in range(NB)
            ]

        spot_rows, high_rows, low_rows = (
            wide_row(spots, small),
            wide_row(highs, BF16),
            wide_row(lows, BF16),
        )
        count = lax.broadcasted_iota(jnp.int32, (16, LANES), 0).astype(small)
        for first in range(0, WINDOW * LANES, 16):
            key = count + small(first)
            by_high = jnp.zeros((16, LANES), BF16)
            by_low = jnp.zeros((16, LANES), BF16)
            for which in range(NB):
                hit = spot_rows[which] == key
                by_high = jnp.where(hit, high_rows[which], by_high)
                by_low = jnp.where(hit, low_rows[which], by_low)
            part, at = matrix[first // LANES], first % LANES
            part[tile, at : at + 16, 0:LANES] = by_high
            part[tile, at : at + 16, LANES : 2 * LANES] = by_low

    for tile in range(GROUP):
        spread_tile(levels, total, wide, matrix, tile, by_matrix + tile, mix)


def build(state, coef, offset, wet):
    levels, cells = state.shape
    rows = cells // LANES
    total = rows + 2 * HALO
    pitch = total + 2 * PAD
    chunks = total // CHUNK
    span = WINDOW * LANES
    return pl.pallas_call(
        build_kernel,
        grid=(chunks,),
        in_specs=[
            pl.BlockSpec(state.shape, lambda i: (0, 0)),
            pl.BlockSpec(coef.shape, lambda i: (0, 0, 0)),
            pl.BlockSpec(offset.shape, lambda i: (0, 0, 0)),
            pl.BlockSpec(wet.shape, lambda i: (0, 0)),
        ],
        out_specs=[
            pl.BlockSpec(((levels + 1) * total, LANES), lambda i: (0, 0)),
            *[pl.BlockSpec((GROUP, LANES, 2 * LANES), lambda i: (i, 0, 0))] * WINDOW,
        ],
        out_shape=[
            jax.ShapeDtypeStruct(((levels + 1) * total, LANES), F32),
            *[jax.ShapeDtypeStruct((chunks * GROUP, LANES, 2 * LANES), BF16)] * WINDOW,
        ],
        scratch_shapes=[
            pltpu.VMEM((levels * pitch, LANES), F32),
            pltpu.VMEM((2 * levels, pitch * LANES), BF16),
            pltpu.VMEM((NB, GROUP, LANES), jnp.int32),
            pltpu.VMEM((NB, GROUP, LANES), F32),
            pltpu.VMEM((NB, GROUP, LANES), F32),
        ],
        compiler_params=pltpu.CompilerParams(vmem_limit_bytes=56 * MIB),
        cost_estimate=pl.CostEstimate(
            flops=2 * chunks * GROUP * 2 * levels * span * 2 * LANES,
            bytes_accessed=80 * MIB,
            transcendentals=0,
        ),
        name="build",
    )(state, coef, offset, wet)


def prepare_kernel(
    state, coef, vert, offset_far, low_far, high_far, *refs
):
    far, (column, edge, inv, from_up, from_down, lanes, codes, coefs, keep, *refs) = (
        refs[:EARLY],
        refs[EARLY:],
    )
    matrix, (verts, low, high, packed, copied) = refs[:EARLY], refs[EARLY:]
    pack_copies = [
        pltpu.make_async_copy(source, target, packed.at[index])
        for index, (source, target) in enumerate(
            (
                (low_far, low),
                (high_far, high),
                (offset_far, lanes.at[:, pl.ds(HALO, state.shape[1] // LANES), :]),
            )
        )
    ]
    matrix_copies = [
        pltpu.make_async_copy(far[reach], matrix[reach], copied.at[reach])
        for reach in range(EARLY)
    ]
    for copy in pack_copies:
        copy.start()
    levels = state.shape[0]
    rows = state.shape[1] // LANES
    total = rows + 2 * HALO
    pitch = column.shape[0] // levels
    inner = levels - 1
    pieces = levels * GROUP

    main = slice(HALO, HALO + rows)
    coefs[:, main, :] = coef[...]
    verts[:, main, :] = vert[...]

    @pl.loop(0, rows, unroll=8)
    def _(row):
        state_rows(state, column, row)

    for copy in pack_copies:
        copy.wait()
    for copy in matrix_copies:
        copy.start()
    for pack, first in ((low, 0), (high, total - HALO)):
        for level in range(levels):
            at = level * pitch + PAD + first
            column[at : at + HALO, :] = pack[level * HALO : (level + 1) * HALO, :]
        here = slice(first, first + HALO)
        at = levels * HALO
        for out, count in ((coefs, NB), (lanes, NB), (verts, inner)):
            for index in range(count):
                out[index, here, :] = pack[at : at + HALO, :].astype(out.dtype)
                at += HALO
        to = 4 * pieces + (0 if first == 0 else HALO)
        edge[to : to + HALO, :] = pack[at : at + HALO, :] * force_scale

    @pl.loop(0, total // GROUP)
    def _(group):
        here = pl.ds(pl.multiple_of(group * GROUP, GROUP), GROUP)
        left = 1.0
        for which in range(NB):
            spot = spots_of(lanes[which, here, :])
            lanes[which, here, :] = lane_of(spot)
            codes[which, here, :] = code_of(spot)
            left = left - coefs[which, here, :]
        keep[here, :] = left
        upper = jnp.zeros((GROUP, LANES), F32)
        carried = jnp.zeros((GROUP, LANES), F32)
        for level in range(levels):
            lower = verts[level, here, :] if level < inner else jnp.zeros((GROUP, LANES), F32)
            pivot = (1.0 + upper + lower) - upper * carried
            inverse = 1.0 / pivot
            carried = lower * inverse
            inv[level, here, :] = inverse
            from_up[level, here, :] = upper * inverse
            from_down[level, here, :] = carried
            upper = lower

    @pl.loop(0, 4)
    def _(index):
        row = edge_row(index, total)
        here = pl.ds(row, GROUP)

        def terms(which):
            return lanes[which, here, :], codes[which, here, :], coefs[which, here, :]

        spread_group(levels, total, column, row, terms, edge, index * pieces, GROUP)

    for copy in matrix_copies:
        copy.wait()


def prepare(state, coef, offset, vert, low, high, matrix):
    levels, cells = state.shape
    rows = cells // LANES
    total = rows + 2 * HALO
    pitch = total + 2 * PAD
    level_shape = pltpu.VMEM((levels, total, LANES), F32)
    index_shape = pltpu.VMEM((NB, total, LANES), jnp.int32)
    near = pl.BlockSpec(memory_space=pltpu.VMEM)
    far = pl.BlockSpec(memory_space=pltpu.HBM)
    offset, low, high, *matrix = [
        pltpu.with_memory_space_constraint(part, pltpu.HBM)
        for part in (offset, low, high, *matrix)
    ]
    return pl.pallas_call(
        prepare_kernel,
        out_shape=[
            pltpu.VMEM((levels * pitch, LANES), F32),
            pltpu.VMEM((4 * levels * GROUP + 2 * HALO, LANES), F32),
            level_shape,
            level_shape,
            level_shape,
            index_shape,
            index_shape,
            pltpu.VMEM((NB, total, LANES), F32),
            pltpu.VMEM((total, LANES), F32),
            *[pltpu.VMEM(part.shape, part.dtype) for part in matrix],
        ],
        in_specs=[near] * 3 + [far] * (3 + EARLY),
        out_specs=[near] * (9 + EARLY),
        scratch_shapes=[
            pltpu.VMEM((levels - 1, total, LANES), F32),
            pltpu.VMEM(low.shape, F32),
            pltpu.VMEM(high.shape, F32),
            pltpu.SemaphoreType.DMA((3,)),
            pltpu.SemaphoreType.DMA((EARLY,)),
        ],
        compiler_params=pltpu.CompilerParams(vmem_limit_bytes=24 * MIB),
        cost_estimate=pl.CostEstimate(flops=0, bytes_accessed=16 * MIB, transcendentals=0),
        name="prepare",
    )(state, coef, vert, offset, low, high, *matrix)


def interval_kernel(
    width, early, column, edge, inv, from_up, from_down, lanes, codes, coefs, keep, *refs
):
    matrix, refs = refs[:EARLY], refs[EARLY:]
    imported, low, high, refs = *refs[:3], refs[3:]
    late_far, (state_out, imported_out, *refs) = refs[: WINDOW - EARLY], refs[WINDOW - EARLY :]
    cells, mixed, wide, force, flat, wets, copied, *late = refs
    matrix = (*matrix, *late)
    late_copies = [
        pltpu.make_async_copy(source, part, copied.at[index])
        for index, (source, part) in enumerate(zip(late_far, late))
    ]
    for copy in late_copies:
        copy.start()
    levels, total = inv.shape[0], inv.shape[1]
    rows = total - 2 * HALO
    pitch = column.shape[0] // levels
    chunks = total // CHUNK

    pieces = levels * GROUP
    wets[...] = early[levels * total : (levels + 1) * total, :]
    wets[0:HALO, :] = edge[4 * pieces : 4 * pieces + HALO, :]
    wets[HALO + rows : total, :] = edge[4 * pieces + HALO : 4 * pieces + 2 * HALO, :]
    force[:, 0:HALO, :] = low[...]
    force[:, HALO : HALO + rows, :] = imported[...]
    force[:, HALO + rows : total, :] = high[...]
    for field in range(width):
        flat[pl.ds(field * rows, rows), :] = imported[field]

    @pl.loop(0, rows, unroll=8)
    def _(row):
        here = pl.ds(pl.multiple_of(row * LANES, LANES), LANES)
        imported_out[:, here] = flat[pl.ds(row, width, stride=rows), :]

    def from_mixed(level, group, row):
        return mixed[pl.ds(level * total + row, GROUP), :]

    def solve(chunk, source, spread_sum, out, wide, groups=(0, 1)):
        for group in groups:
            row = pl.multiple_of(chunk * CHUNK + group * GROUP, GROUP)
            here = pl.ds(row, GROUP)
            left = keep[here, :]
            wet = wets[here, :]
            partial = []
            for level in range(levels):
                value = left * source[pl.ds(level * pitch + PAD + row, GROUP), :]
                value = value + spread_sum(level, group, row)
                if level < width:
                    value = value + force[level, here, :] * wet
                value = value * inv[level, here, :]
                if level:
                    value = value + from_up[level, here, :] * partial[-1]
                partial.append(value)
            following = partial[-1]
            out[pl.ds((levels - 1) * pitch + PAD + row, GROUP), :] = following
            for level in range(levels - 2, -1, -1):
                following = partial[level] + from_down[level, here, :] * following
                out[pl.ds(level * pitch + PAD + row, GROUP), :] = following
        for row in range(CHUNK if wide is not None else 0):
            to_lanes(levels, out, wide, chunk * CHUNK + row)

    def spread(chunk, source, wide, gathers=True):
        by_matrix, by_gather = group_rows(chunk, chunks)
        for tile in range(GROUP):
            spread_tile(
                levels, total, wide, matrix, chunk * GROUP + tile, by_matrix + tile, mixed
            )
        if not gathers:
            return
        here = pl.ds(by_gather, GROUP)

        def terms(which):
            return lanes[which, here, :], codes[which, here, :], coefs[which, here, :]

        spread_group(levels, total, source, by_gather, terms, mixed)

    def from_early(level, group, row):
        return early[pl.ds(level * total + row, GROUP), :]

    def from_edge(last, level, group, row):
        return edge[pl.ds((2 * last + group) * pieces + level * GROUP, GROUP), :]

    solve(0, column, functools.partial(from_edge, 0), cells, wide)

    @pl.loop(1, chunks - 1)
    def _(chunk):
        solve(chunk, column, from_early, cells, wide)

    solve(chunks - 1, column, functools.partial(from_edge, 1), cells, wide)
    for copy in late_copies:
        copy.wait()

    @pl.loop(1, STEPS - 1)
    def _(step):
        for chunk in range(chunks):
            spread(jnp.int32(chunk), cells, wide)
        for chunk in range(chunks):
            solve(chunk, cells, from_mixed, cells, wide)

    for chunk in range(chunks):
        spread(jnp.int32(chunk), cells, wide, 0 < chunk < chunks - 1)
    for chunk in range(chunks):
        groups = (1,) if chunk == 0 else (0,) if chunk == chunks - 1 else (0, 1)
        solve(chunk, cells, from_mixed, cells, None, groups)

    @pl.loop(0, rows, unroll=8)
    def _(row):
        here = pl.ds(pl.multiple_of(row * LANES, LANES), LANES)
        for level in range(0, levels, 8):
            at = level * pitch + PAD + HALO + row
            state_out[level : level + 8, here] = cells[pl.ds(at, 8, stride=pitch), :]


def interval(late, early, column, edge, inv, *rest):
    levels, total = inv.shape[0], inv.shape[1]
    pitch = column.shape[0] // levels
    width, rows = rest[-3].shape[0], rest[-3].shape[1]
    operands = (early, column, edge, inv, *rest)
    late = [pltpu.with_memory_space_constraint(part, pltpu.HBM) for part in late]
    return pl.pallas_call(
        functools.partial(interval_kernel, width),
        out_shape=[
            jax.ShapeDtypeStruct((levels, rows * LANES), F32),
            jax.ShapeDtypeStruct((width, rows * LANES), F32),
        ],
        in_specs=[pl.BlockSpec(memory_space=pltpu.VMEM)] * len(operands)
        + [pl.BlockSpec(memory_space=pltpu.HBM)] * len(late),
        out_specs=[pl.BlockSpec(memory_space=pltpu.VMEM)] * 2,
        scratch_shapes=[
            pltpu.VMEM(column.shape, F32),
            pltpu.VMEM((levels * total, LANES), F32),
            pltpu.VMEM((2 * levels, pitch * LANES), BF16),
            pltpu.VMEM((width, total, LANES), F32),
            pltpu.VMEM((width * rows, LANES), F32),
            pltpu.VMEM((total, LANES), F32),
            pltpu.SemaphoreType.DMA((len(late),)),
            *[pltpu.VMEM(part.shape, part.dtype) for part in late],
        ],
        compiler_params=pltpu.CompilerParams(vmem_limit_bytes=24 * MIB),
        name="interval",
    )(*operands, *late)


def local(
    state,
    export_fields,
    remap_weights,
    routes,
    target_block,
    source_block,
    wet_mask,
    edge_coeff,
    edge_offset,
    vert_coeff,
):
    owners = lax.axis_size("dom")
    comps = lax.axis_size("comp")
    cells = state.shape[2]
    block_count = remap_weights.shape[1]
    capacity = max(2, 2 * block_count // owners)
    width = export_fields.shape[1]
    rows = cells // LANES
    me = lax.axis_index("dom").astype(jnp.int32)[None]
    coef = edge_coeff[0].reshape(-1, rows, LANES)
    offset = edge_offset[0].reshape(-1, rows, LANES)
    vert = vert_coeff[0].reshape(-1, rows, LANES)
    wet = wet_mask.reshape(rows, LANES)

    values, low, high = remap(
        routes[0, :, 0],
        target_block[0],
        source_block[0],
        me,
        export_fields[0],
        remap_weights[0],
        state[0],
        (coef, offset, vert, wet),
        owners,
        capacity,
    )
    values = lax.all_to_all(values, "dom", split_axis=0, concat_axis=0, tiled=True)

    forward = [(i, (i + 1) % owners) for i in range(owners)]
    backward = [(target, source) for source, target in forward]
    low = lax.ppermute(low, "dom", forward)
    high = lax.ppermute(high, "dom", backward)
    built = build(state[0], coef, offset, wet)
    values, built, low, high = lax.optimization_barrier((values, built, low, high))
    early, *matrix = built
    early = pltpu.with_memory_space_constraint(early, pltpu.VMEM)

    pitch = capacity * width + 8
    summed, first_rows, last_rows = assemble(
        values.reshape(owners * pitch, LANES), owners, capacity, width, rows
    )

    def across(value, shift):
        pairs = [
            (comp * owners + dom, (comp + 1) % comps * owners + (dom + shift) % owners)
            for comp in range(comps)
            for dom in range(owners)
        ]
        return lax.ppermute(value, ("comp", "dom"), pairs)

    imported = across(summed, 0)
    from_low = across(last_rows, 1)
    from_high = across(first_rows, -1)
    prepared = prepare(state[0], coef, offset, vert, low, high, matrix[:EARLY])
    new_state, imported = interval(
        matrix[EARLY:], early, *prepared, imported, from_low, from_high
    )
    return (new_state[None], imported[None])


def solution(mesh):
    placed = (
        P("comp", None, "dom"),
        P("comp", None, "dom"),
        P("comp", "dom", None, None),
        P("comp", "dom", None),
        P("comp", "dom"),
        P("comp", "dom"),
        P("comp", "dom"),
        P("comp", None, "dom"),
        P("comp", None, "dom"),
        P("comp", None, "dom"),
    )
    return jax.shard_map(
        local,
        mesh=mesh,
        in_specs=placed,
        out_specs=(P("comp", None, "dom"), P("comp", None, "dom")),
        check_vma=False,
    )
```
